256 devices in a mesh: region: 8 (over z_hi, core), tile: 32 (over y, x, z_lo).
Axes of the slice: x: 4, y: 4, z: 8 (z_hi: 4, z_lo: 2; z = z_hi * 2 + z_lo), core: 2. Of those that a mesh axis runs over, the one named last changes fastest.
Arguments:
- tangent: float32 [8, 32, 2, 64, 900], P('region', 'tile'), may hold values from -6 to 6
- adjoint: float32 [8, 32, 2, 64, 900], P('region', 'tile'), may hold values from -6 to 6
- reference_uppermost_tracers: float32 [8, 32, 2, 900], P('region', 'tile'), may hold values from -1 to 1.5
- velocity: float32 [8, 32, 2, 64, 900], P('region', 'tile'), may hold values from -1.5 to 1.5
- kappa: float32 [8, 32, 63, 900], P('region', 'tile'), may hold values from 0.025 to 1600
- depth_levels: int32 [8, 32, 900], P('region', 'tile'), may hold values from 0 to 64
- forcing: float32 [8, 131072], P(None, 'region'), may hold values from -4 to 4
- forcing_point: int32 [8, 32, 900], P('region', 'tile'), may hold values from 0 to 131071
- partner_edge: int32 [8, 32, 4], P('region', 'tile'), may hold values from 0 to 127, as said below
- edge_flip: int32 [8, 32, 4], P('region', 'tile'), may hold values from 0 to 1
Outputs:
- tangent_next: float32 [8, 32, 2, 64, 900], P('region', 'tile')
- adjoint_prev: float32 [8, 32, 2, 64, 900], P('region', 'tile')
The draws below stay inside these ranges and needn't reach their ends.
Inputs may be any that keep to these rules, and one draw needn't show every extreme that they name: partner_edge[r, t, s] names an edge of the same region; partner of partner is the edge itself, no edge names itself, and edge_flip agrees on both edges of a pair. The side 0 edge of each slot pairs with the side 1 edge of the same slot. Every side 2 edge pairs with the side 2 edge of another slot, and every side 3 edge pairs with the side 3 edge of another slot.
All inputs are finite; a program needn't handle non-finite values.
Results may differ from the reference program's by a relative error of at most 0.0003.
Values sent between devices are 32-bit elements; how exact they have to be, the bound alone decides.
No kernel may reach another device: no remote copies, remote signals or barrier semaphores. Data moves between devices by JAX's collectives and lax.ppermute only.
A program may use at most 192 MiB of HBM per device.

```python
import jax
import jax.numpy as jnp
from jax import lax

SIDE = 30
Z = 64
FIELDS = 8
TILES_DEV = 1
SLOTS = 32
FPTS = 131072
N_REGION = 8


def pairing_table(key):
    blocks = SLOTS // TILES_DEV

    def one_region(region):
        region_key = jax.random.fold_in(key, region)
        block_ids = jnp.arange(blocks, dtype=jnp.int32)
        within = jnp.arange(TILES_DEV, dtype=jnp.int32)
        slot_ids = (block_ids[:, None] * TILES_DEV + within[None, :]).reshape(-1)
        block_of = slot_ids // TILES_DEV
        place = slot_ids % TILES_DEV
        west_slot = block_of * TILES_DEV + (place - 1) % TILES_DEV
        south_slot_reg = (block_of - 1) % blocks * TILES_DEV + place
        west_mate = 4 * west_slot + 1
        east_mate = 4 * (block_of * TILES_DEV + (place + 1) % TILES_DEV) + 0
        south_mate = 4 * south_slot_reg + 3
        north_mate = 4 * ((block_of + 1) % blocks * TILES_DEV + place) + 2
        partner = jnp.stack([west_mate, east_mate, south_mate, north_mate], axis=1).astype(jnp.int32)
        east_bits = jax.random.randint(jax.random.fold_in(region_key, 23), (SLOTS,), 0, 2).astype(jnp.int32)
        north_bits = jax.random.randint(jax.random.fold_in(region_key, 29), (SLOTS,), 0, 2).astype(jnp.int32)
        flips = jnp.stack([east_bits[west_slot], east_bits, north_bits[south_slot_reg], north_bits], axis=1).astype(jnp.int32)
        columns = jax.random.randint(jax.random.fold_in(region_key, 17), (blocks,), 0, TILES_DEV).astype(jnp.int32)
        order = jax.random.permutation(jax.random.fold_in(region_key, 11), blocks).astype(jnp.int32)
        first = order[0::2]
        second = order[1::2]
        mate = jnp.zeros((blocks,), jnp.int32).at[first].set(second).at[second].set(first)
        face_bits = jax.random.randint(jax.random.fold_in(region_key, 31), (blocks,), 0, 2).astype(jnp.int32)
        pair_bit = face_bits[jnp.minimum(block_ids, mate)]
        south_slot = block_ids * TILES_DEV + columns
        north_slot = (block_ids - 1) % blocks * TILES_DEV + columns
        partner = partner.at[south_slot, 2].set(4 * south_slot[mate] + 2)
        partner = partner.at[north_slot, 3].set(4 * north_slot[mate] + 3)
        north_pair_bit = face_bits[jnp.minimum(block_ids, mate) + blocks * 0]
        flips = flips.at[south_slot, 2].set(pair_bit).at[north_slot, 3].set(north_pair_bit)
        return (partner, flips)
    return jax.vmap(one_region)(jnp.arange(N_REGION, dtype=jnp.int32))


def draw_partner_edge(key, part):
    return pairing_table(jax.random.fold_in(key, 101))[0]


def draw_edge_flip(key, part):
    return pairing_table(jax.random.fold_in(key, 101))[1]


def draw_kappa(key, part):
    key = jax.random.fold_in(key, 7)
    lowest = 0.05
    highest = 400.0
    column_base = jax.random.uniform(jax.random.fold_in(key, 1), (N_REGION, SLOTS, 1, SIDE * SIDE), jnp.float32, jnp.log(lowest), jnp.log(highest))
    roughness = jax.random.uniform(jax.random.fold_in(key, 2), (N_REGION, SLOTS, Z - 1, SIDE * SIDE), jnp.float32, jnp.log(0.5), jnp.log(2.0))
    return jnp.clip(jnp.exp(column_base + roughness), 0.025, 1600.0).astype(jnp.float32)


def plant(drawn, stream_key, smallest, largest):
    spot = [jax.random.randint(jax.random.fold_in(stream_key, axis), (), 0, length) for axis, length in enumerate(drawn.shape)]
    widest = drawn.shape.index(max(drawn.shape))
    next_to = spot[:widest] + [(spot[widest] + 1) % drawn.shape[widest]] + spot[widest + 1:]
    return drawn.at[tuple(spot)].set(smallest).at[tuple(next_to)].set(largest)


def level_of(key, extent, split, low, high):
    factor_of = 1.0
    for dim, blocks in split:
        heights = jax.random.uniform(jax.random.fold_in(jax.random.fold_in(key, 6), dim), (blocks,), jnp.float32, low / len(split), high / len(split))
        factor_of = factor_of * jnp.repeat(jnp.exp(heights), extent[dim] // blocks).reshape((-1,) + (1,) * (len(extent) - 1 - dim))
    return factor_of


def noise(stream_key, extent, scale, reach, cuts=(), kind=jnp.bfloat16):
    array = scale * jax.random.normal(stream_key, extent, jnp.float32)
    if cuts:
        array = array * level_of(stream_key, extent, cuts, -0.22, 0.18)
    return jnp.clip(array, -reach, reach).astype(kind)


def setup_inputs(seed: int = 0) -> dict:
    key_list = jax.random.split(jax.random.key(seed), 11)
    tangent = noise(key_list[0], (N_REGION, SLOTS, 2, Z, SIDE * SIDE), 1.0, 6.0, ((0, 8), (1, 32)), jnp.float32)
    adjoint = noise(key_list[1], (N_REGION, SLOTS, 2, Z, SIDE * SIDE), 1.0, 6.0, ((0, 8), (1, 32)), jnp.float32)
    reference_uppermost_tracers = jnp.clip(-1.0 + 2.5 * jax.random.uniform(key_list[2], (N_REGION, SLOTS, 2, SIDE * SIDE), jnp.float32) ** level_of(key_list[2], (N_REGION, SLOTS, 2, SIDE * SIDE), ((0, 8), (1, 32)), -0.2, 0.2), -1.0, 1.5)
    velocity = noise(key_list[3], (N_REGION, SLOTS, 2, Z, SIDE * SIDE), 0.3, 1.5, ((0, 8), (1, 32)), jnp.float32)
    kappa = draw_kappa(jax.random.fold_in(key_list[10], 71), 0)
    depth_levels = plant(jax.random.randint(key_list[5], (N_REGION, SLOTS, SIDE * SIDE), 0, Z + 1), jax.random.fold_in(key_list[5], 1), 0, Z).astype(jnp.int32)
    forcing = noise(key_list[6], (FIELDS, FPTS), 1.0, 4.0, ((1, 8),), jnp.float32)
    forcing_point = plant(jax.random.randint(key_list[7], (N_REGION, SLOTS, SIDE * SIDE), 0, FPTS), jax.random.fold_in(key_list[7], 1), 0, FPTS - 1).astype(jnp.int32)
    partner_edge = draw_partner_edge(jax.random.fold_in(key_list[10], 71), 0)
    edge_flip = draw_edge_flip(jax.random.fold_in(key_list[10], 71), 0)
    return {"tangent": tangent, "adjoint": adjoint, "reference_uppermost_tracers": reference_uppermost_tracers, "velocity": velocity, "kappa": kappa, "depth_levels": depth_levels, "forcing": forcing, "forcing_point": forcing_point, "partner_edge": partner_edge, "edge_flip": edge_flip}


diffusion = 0.2

def grid_masks():
    position = jnp.arange(SIDE * SIDE, dtype=jnp.int32)
    return (position % SIDE, position // SIDE)

def edge_rows(west_src, east_src, south_src, north_src):
    slot_count = west_src.shape[0]
    shaped = lambda source: source.reshape(slot_count, 2 * Z, SIDE, SIDE)
    stacked = jnp.stack([shaped(west_src)[:, :, :, 0], shaped(east_src)[:, :, :, SIDE - 1], shaped(south_src)[:, :, 0, :], shaped(north_src)[:, :, SIDE - 1, :]], axis=1)
    return jnp.transpose(stacked, (0, 1, 3, 2)).reshape(slot_count * 4, SIDE, 2 * Z)

def take_partner(gathered, partner_edge, edge_flip):
    slot_count = partner_edge.shape[0]
    chosen = jnp.take(gathered, partner_edge.reshape(-1), axis=0)
    flipped = jnp.where(edge_flip.reshape(-1)[:, None, None] == 1, chosen[:, ::-1, :], chosen)
    return jnp.transpose(flipped.reshape(slot_count, 4, SIDE, 2 * Z), (0, 1, 3, 2)).reshape(slot_count, 4, 2, Z, SIDE)

def spread(rim_values):
    west_full = jnp.repeat(rim_values[:, 0], SIDE, axis=-1)
    east_full = jnp.repeat(rim_values[:, 1], SIDE, axis=-1)
    south_full = jnp.tile(rim_values[:, 2], (1, 1, 1, SIDE))
    north_full = jnp.tile(rim_values[:, 3], (1, 1, 1, SIDE))
    return (west_full, east_full, south_full, north_full)

def horizontal(tracer, rim_values, velocity, wetness):
    column, row_index = grid_masks()
    west_full, east_full, south_full, north_full = spread(rim_values)
    from_east = jnp.where(column == SIDE - 1, east_full, jnp.roll(tracer, -1, axis=-1))
    from_west = jnp.where(column == 0, west_full, jnp.roll(tracer, 1, axis=-1))
    from_north = jnp.where(row_index == SIDE - 1, north_full, jnp.roll(tracer, -SIDE, axis=-1))
    from_south = jnp.where(row_index == 0, south_full, jnp.roll(tracer, SIDE, axis=-1))
    along_x = velocity[:, 0:1]
    along_y = velocity[:, 1:2]
    mixed_terms = (1.0 - 4.0 * diffusion) * tracer + (diffusion - 0.5 * along_x) * from_east + (diffusion + 0.5 * along_x) * from_west
    mixed_terms = mixed_terms + (diffusion - 0.5 * along_y) * from_north + (diffusion + 0.5 * along_y) * from_south
    return wetness * mixed_terms

def surface_terms(reference_uppermost_tracers, forcing_cells, uppermost_ocean_indicator):
    wind_east, wind_north, air_temp, moisture_content, precipitation_amount, continental_discharge, pressure, ice_cover = [forcing_cells[number] for number in range(8)]
    airflow_magnitude = jnp.sqrt(wind_east * wind_east + wind_north * wind_north + 1.0)
    seawater_mass_per_volume = jnp.exp(0.3 * (pressure - air_temp))
    icefree_share = 1.0 / (1.0 + jnp.exp(ice_cover))
    transported_quantity = icefree_share * seawater_mass_per_volume * airflow_magnitude
    vapour_capacity_moisture = jnp.exp(0.5 * reference_uppermost_tracers[:, 0] - 0.2 * pressure)
    vapour_capacity_derivative = 0.5 * vapour_capacity_moisture
    precipitation_minus_evaporation = 0.5 * transported_quantity * (vapour_capacity_moisture - moisture_content) - precipitation_amount - continental_discharge
    thermal_diagonal_coupling = -(0.5 * transported_quantity + 0.5 * transported_quantity * vapour_capacity_derivative) * uppermost_ocean_indicator
    haline_thermal_coupling = 0.5 * reference_uppermost_tracers[:, 1] * transported_quantity * vapour_capacity_derivative * uppermost_ocean_indicator
    salt_self = precipitation_minus_evaporation * uppermost_ocean_indicator
    return (thermal_diagonal_coupling, haline_thermal_coupling, salt_self)

def vertical_solve(right_side, coupling):
    slot_count = right_side.shape[0]
    edge_zero = jnp.zeros((slot_count, 1, SIDE * SIDE), jnp.float32)
    upper_link = jnp.concatenate([edge_zero, coupling], axis=1)
    lower_link = jnp.concatenate([coupling, edge_zero], axis=1)
    centre = 1.0 + upper_link + lower_link
    stacked = (jnp.moveaxis(centre, 1, 0)[:, :, None], jnp.moveaxis(upper_link, 1, 0)[:, :, None], jnp.moveaxis(lower_link, 1, 0)[:, :, None], jnp.moveaxis(right_side, 2, 0))

    def eliminate(carry, inputs):
        factor_prev, partial_prev = carry
        centre_here, upper_here, lower_here, right_here = inputs
        divisor = centre_here + upper_here * factor_prev
        factor = -lower_here / divisor
        partial_value = (right_here + upper_here * partial_prev) / divisor
        return ((factor, partial_value), (factor, partial_value))
    initial = (jnp.zeros((slot_count, 1, SIDE * SIDE), jnp.float32), jnp.zeros((slot_count, 2, SIDE * SIDE), jnp.float32))
    unused, (factors, partials) = lax.scan(eliminate, initial, stacked)

    def substitute(carry, inputs):
        factor, partial_value = inputs
        result = partial_value - factor * carry
        return (result, result)
    unused_last, solved = lax.scan(substitute, jnp.zeros((slot_count, 2, SIDE * SIDE), jnp.float32), (factors, partials), reverse=True)
    return jnp.moveaxis(solved, 0, 2)

def region_step(tangent, adjoint, reference_uppermost_tracers, velocity, kappa, depth_levels, forcing_point, partner_edge, edge_flip, forcing):
    levels = jnp.arange(Z, dtype=jnp.int32)
    wet_levels = (levels[None, :, None] < depth_levels[:, None, :]).astype(jnp.float32)
    wetness = wet_levels[:, None]
    coupling = kappa * wet_levels[:, :-1] * wet_levels[:, 1:]
    forcing_cells = jnp.take(forcing, forcing_point, axis=1)
    thermal_diagonal_coupling, haline_thermal_coupling, salt_self = surface_terms(reference_uppermost_tracers, forcing_cells, wet_levels[:, 0])

    def step(tracer):
        masked = tracer * wetness
        edges_all = edge_rows(masked, masked, masked, masked)
        rim_values = take_partner(edges_all, partner_edge, edge_flip)
        right_side = horizontal(masked, rim_values, velocity, wetness)
        top_heat = thermal_diagonal_coupling * masked[:, 0, 0]
        top_salt = haline_thermal_coupling * masked[:, 0, 0] + salt_self * masked[:, 1, 0]
        right_side = right_side.at[:, 0, 0].add(top_heat).at[:, 1, 0].add(top_salt)
        return vertical_solve(right_side, coupling)
    forward_out, pullback = jax.vjp(step, tangent)
    return (forward_out, pullback(adjoint)[0])

def reference(tangent, adjoint, reference_uppermost_tracers, velocity, kappa, depth_levels, forcing, forcing_point, partner_edge, edge_flip):

    def one_region(items):
        return region_step(*items, forcing)
    return lax.map(one_region, (tangent, adjoint, reference_uppermost_tracers, velocity, kappa, depth_levels, forcing_point, partner_edge, edge_flip))
```

```python
import jax
import jax.numpy as jnp
from jax import lax
from jax.experimental import pallas as pl
from jax.experimental.pallas import tpu as pltpu
from jax.sharding import PartitionSpec as P

SIDE = 30
Z = 64
CELLS = SIDE * SIDE
WIDE = 1024
CHUNKS = WIDE // 128
GROUPS = Z // 8
D = 0.2
CENTRE = 1.0 - 4.0 * D
F32 = jnp.float32
VMEM_LIMIT = 48 * 1024 * 1024


def lanes(rows, width=WIDE):
    return lax.broadcasted_iota(jnp.int32, (rows, width), 1)


def split(row):
    return [row[:, 128 * c : 128 * c + 128] for c in range(CHUNKS)]


def roll(value, shift):
    return pltpu.roll(value, shift % value.shape[-1], value.ndim - 1)


def grid_masks(rows=1):
    cell = lanes(rows)
    y = lax.shift_right_logical(cell * 2185, 16)
    x = cell - y * SIDE
    return x == 0, x == SIDE - 1, y == 0, y == SIDE - 1


def mirrored(value):
    back = 127 - lanes(value.shape[0], 128)
    parts = [jnp.take_along_axis(part, back, axis=1) for part in split(value)]
    return roll(jnp.concatenate(parts[::-1], axis=1), CELLS)


def table_kernel(forcing_ref, table_ref):
    wu, wv, ta, qa, pr, ro, ps, ic = [
        forcing_ref[pl.ds(field, 128, stride=8), :] for field in range(8)
    ]
    speed = jnp.sqrt(wu * wu + wv * wv + 1.0)
    carrier = jnp.exp(0.3 * (ps - ta)) * speed / (1.0 + jnp.exp(ic))
    table_ref[0:128, :] = carrier
    table_ref[128:256, :] = carrier * jnp.exp(-0.2 * ps)
    table_ref[256:384, :] = 0.5 * carrier * qa + pr + ro


def lookup_kernel(own_ref, mate_ref, q0, q1, q2, q3, a0, a1, a2, a3, pieces, ask):
    band = lax.axis_index("region")
    for number, ref in enumerate((own_ref, mate_ref)):
        value = ref[...]
        coarse = value.astype(jnp.bfloat16)
        pieces[384 * number : 384 * number + 384, 0:128] = coarse
        pieces[384 * number : 384 * number + 384, 128:256] = (
            value - coarse.astype(F32)
        ).astype(jnp.bfloat16)
    base_own = band * 128
    base_mate = (band + 1 - 2 * lax.rem(band, 2)) * 128
    low = jnp.bitwise_and(lax.broadcasted_iota(jnp.int32, (256, 256), 0), 127)
    high = lax.broadcasted_iota(jnp.int32, (128, 256), 0)
    for q_ref, a_ref in ((q0, a0), (q1, a1), (q2, a2), (q3, a3)):
        ask[...] = jnp.zeros((1, WIDE), jnp.int32)
        ask[:, 0:CELLS] = q_ref[0]
        for part in range(4):
            point = ask[:, 256 * part : 256 * part + 256]
            onehot = (low == jnp.bitwise_and(point, 127)).astype(jnp.bfloat16)
            found = jnp.dot(pieces[...], onehot, preferred_element_type=F32)
            row = lax.shift_right_logical(point, 7)
            here = high == row - base_own
            there = high == row - base_mate
            for field in range(3):
                picked = jnp.where(here, found[128 * field : 128 * field + 128], 0.0)
                picked = picked + jnp.where(
                    there, found[384 + 128 * field : 512 + 128 * field], 0.0
                )
                total = jnp.sum(picked, axis=0, keepdims=True)
                at = 8 * field + 2 * part
                a_ref[at : at + 1, :] = total[:, 0:128]
                a_ref[at + 1 : at + 2, :] = total[:, 128:256]


def main_kernel(
    partner_ref, flip_ref, tan_ref, adj_ref, vel_ref, kap_ref, depth_ref,
    edge_ref, rhs_ref, back_ref, rim_ref, top_ref, link_ref, inv_ref,
    coup, given, part, solved,
):
    cell = lanes(1)
    depth = jnp.where(cell < CELLS, depth_ref[...], 0)
    sub = lax.broadcasted_iota(jnp.int32, (8, WIDE), 0)

    def relayout(i, carry):
        rows = pl.ds(pl.multiple_of(8 * i, 8), 8)
        level = sub + 8 * i
        link = jnp.where(level + 1 < depth, kap_ref[rows, :], 0.0)
        at = pl.multiple_of(64 * i, 64)
        sources = (link, adj_ref[0, rows, :], adj_ref[1, rows, :])
        for target, value in enumerate(sources):
            for c, piece in enumerate(split(value)):
                where = pl.ds(at + 8 * c, 8)
                if target == 0:
                    coup[where, :] = piece
                else:
                    given[target - 1, where, :] = piece
        return carry

    lax.fori_loop(0, GROUPS, relayout, 0)

    def forward(i, carry):
        e, y_t, y_s, m = carry
        for s in range(8):
            strided = pl.ds(64 * i + s, 8, stride=8)
            packed = pl.ds(pl.multiple_of(64 * i + 8 * s, 8), 8)
            link = coup[strided, :]
            inv = 1.0 / (e + link)
            y_t = given[0, strided, :] + m * y_t
            y_s = given[1, strided, :] + m * y_s
            m = link * inv
            e = 1.0 + m * e
            inv_ref[packed, :] = inv
            link_ref[packed, :] = m
            part[0, packed, :] = y_t * inv
            part[1, packed, :] = y_s * inv
        return e, y_t, y_s, m

    zero = jnp.zeros((8, 128), F32)
    lax.fori_loop(0, GROUPS, forward, (zero + 1.0, zero, zero, zero))

    def backward(n, carry):
        x_t, x_s = carry
        i = GROUPS - 1 - n
        for s in reversed(range(8)):
            strided = pl.ds(64 * i + s, 8, stride=8)
            packed = pl.ds(pl.multiple_of(64 * i + 8 * s, 8), 8)
            m = link_ref[packed, :]
            x_t = part[0, packed, :] + m * x_t
            x_s = part[1, packed, :] + m * x_s
            solved[0, strided, :] = x_t
            solved[1, strided, :] = x_s
        return x_t, x_s

    x_t, x_s = lax.fori_loop(0, GROUPS, backward, (zero, zero))
    top_ref[16:24, :] = x_t
    top_ref[24:32, :] = x_s

    x0, x29, y0, y29 = grid_masks(8)
    turned = jnp.full((8, WIDE), flip_ref[0, 0] == 1)
    small = lanes(8, 128)
    south, north = flip_ref[0, 2] == 1, flip_ref[0, 3] == 1
    order = small
    for first, turn in ((0, south), (30, north), (60, south), (90, north)):
        inside = jnp.logical_and(small >= first, small < first + SIDE)
        order = jnp.where(
            jnp.logical_and(inside, turn), 2 * first + SIDE - 1 - small, order
        )

    def stencil(i, carry):
        rows = pl.ds(pl.multiple_of(8 * i, 8), 8)
        at = pl.multiple_of(64 * i, 64)
        wet = sub + 8 * i < depth
        half_x, half_y = 0.5 * vel_ref[0, rows, :], 0.5 * vel_ref[1, rows, :]
        to_e, to_w, to_n, to_s = D - half_x, D + half_x, D - half_y, D + half_y
        for t in range(2):
            value = jnp.where(wet, tan_ref[t, rows, :], 0.0)
            image = mirrored(value)
            east = jnp.where(
                x29, jnp.where(turned, image, roll(value, 29)), roll(value, -1)
            )
            west = jnp.where(
                x0, jnp.where(turned, image, roll(value, -29)), roll(value, 1)
            )
            northern = jnp.where(y29, 0.0, roll(value, -SIDE))
            southern = jnp.where(y0, 0.0, roll(value, SIDE))
            mixed = CENTRE * value + to_e * east + to_w * west
            mixed = jnp.where(wet, mixed + to_n * northern + to_s * southern, 0.0)
            for c, piece in enumerate(split(mixed)):
                rhs_ref[t, pl.ds(at + 8 * c, 8), :] = piece

            answer = jnp.concatenate(
                [solved[t, pl.ds(at + 8 * c, 8), :] for c in range(CHUNKS)], axis=1
            )
            answer = jnp.where(wet, answer, 0.0)
            push_e = jnp.where(wet, to_e * answer, 0.0)
            push_w = jnp.where(wet, to_w * answer, 0.0)
            push_n = jnp.where(wet, to_n * answer, 0.0)
            push_s = jnp.where(wet, to_s * answer, 0.0)
            crossing = jnp.where(x29, push_e, push_w)
            image = mirrored(crossing)
            inner = CENTRE * answer
            inner = inner + jnp.where(
                x0, jnp.where(turned, image, roll(crossing, -29)), roll(push_e, 1)
            )
            inner = inner + jnp.where(
                x29, jnp.where(turned, image, roll(crossing, 29)), roll(push_w, -1)
            )
            inner = inner + jnp.where(y0, 0.0, roll(push_n, SIDE))
            inner = inner + jnp.where(y29, 0.0, roll(push_s, -SIDE))
            inner = jnp.where(wet, inner, 0.0)
            for c, piece in enumerate(split(inner)):
                back_ref[t, pl.ds(at + 8 * c, 8), :] = piece

            value, push_s, push_n = split(value), split(push_s), split(push_n)
            upper = small >= 102
            edges = jnp.where(small < 30, value[0], 0.0)
            packs = (
                (roll(jnp.where(upper, value[6], value[7]), 56), 30),
                (roll(push_s[0], 60), 60),
                (roll(jnp.where(upper, push_n[6], push_n[7]), 116), 90),
            )
            for piece, first in packs:
                inside = jnp.logical_and(small >= first, small < first + SIDE)
                edges = jnp.where(inside, piece, edges)
            edges = jnp.take_along_axis(edges, order, axis=1)
            edge_ref[pl.ds(pl.multiple_of(64 * t + 8 * i, 8), 8), :] = edges
        wet, to_n, to_s = split(wet), split(to_n), split(to_s)
        rim = (
            jnp.where(jnp.logical_and(wet[0], small < SIDE), to_s[0], 0.0),
            jnp.where(jnp.logical_and(wet[6], small >= 102), to_n[6], 0.0),
            jnp.where(jnp.logical_and(wet[7], small < 4), to_n[7], 0.0),
        )
        for number, piece in enumerate(rim):
            rim_ref[pl.ds(pl.multiple_of(64 * number + 8 * i, 8), 8), :] = piece
        return carry

    lax.fori_loop(0, GROUPS, stencil, 0)
    wet = 0 < depth
    for t in range(2):
        for c, piece in enumerate(split(jnp.where(wet, tan_ref[t, 0:1, :], 0.0))):
            top_ref[8 * t + c : 8 * t + c + 1, :] = piece
    second = jnp.logical_or(small < 30, jnp.logical_and(small >= 60, small < 90))
    target = jnp.where(
        second,
        lax.shift_right_logical(partner_ref[0, 2], 2),
        lax.shift_right_logical(partner_ref[0, 3], 2),
    )
    edge_ref[128:136, :] = jnp.where(small < 120, target, -1).astype(F32)


def route_kernel(e0, e1, e2, e3, out_ref):
    mine = jnp.bitwise_and(lax.axis_index("tile"), 3)
    sources = (e0, e1, e2, e3)
    goals = [ref[128:129, :].astype(jnp.int32) for ref in sources]
    for b in range(8):
        total = jnp.zeros((128, 128), F32)
        for goal, ref in zip(goals, sources):
            total = jnp.where(goal == 4 * b + mine, ref[0:128, :], total)
        out_ref[b] = total


def finish_kernel(
    edge_ref, rhs_ref, back_ref, rim_ref, top_ref, link_ref, inv_ref,
    r0, r1, r2, r3, depth_ref, base_ref, next_ref, prev_ref,
    right, part, solved, row,
):
    cell = lanes(1)
    depth = jnp.where(cell < CELLS, depth_ref[...], 0)
    for c, piece in enumerate(split(depth)):
        row[0, c : c + 1, :] = piece.astype(F32)
    for t in range(2):
        for c, piece in enumerate(split(base_ref[t : t + 1, :])):
            row[1 + t, c : c + 1, :] = piece
    carrier, scaled, loss = [
        r0[8 * f : 8 * f + 8, :]
        + r1[8 * f : 8 * f + 8, :]
        + r2[8 * f : 8 * f + 8, :]
        + r3[8 * f : 8 * f + 8, :]
        for f in range(3)
    ]
    moist = scaled * jnp.exp(0.5 * row[1])
    wet = row[0] > 0.0
    heat_self = jnp.where(wet, -(0.5 * carrier + 0.25 * moist), 0.0)
    salt_heat = jnp.where(wet, 0.25 * row[2] * moist, 0.0)
    salt_self = jnp.where(wet, 0.5 * moist - loss, 0.0)
    tan_t, tan_s = top_ref[0:8, :], top_ref[8:16, :]
    adj_t, adj_s = top_ref[16:24, :], top_ref[24:32, :]

    small = lanes(8, 128)
    sub = lax.broadcasted_iota(jnp.int32, (8, WIDE), 0)

    def rims(i, carry):
        rows = pl.ds(pl.multiple_of(8 * i, 8), 8)
        at = pl.multiple_of(64 * i, 64)
        wet = split(sub + 8 * i < depth)
        rim = [rim_ref[pl.ds(pl.multiple_of(64 * n + 8 * i, 8), 8), :] for n in range(3)]
        for t in range(2):
            where = pl.ds(pl.multiple_of(64 * t + 8 * i, 8), 8)
            edge = edge_ref[0, where, :]
            for b in range(1, 8):
                edge = edge + edge_ref[b, where, :]
            north = roll(edge, 72)
            from_s, from_n = roll(edge, 68), roll(edge, 12)
            for c in range(CHUNKS):
                put = pl.ds(at + 8 * c, 8)
                value = rhs_ref[t, put, :]
                if c == 0:
                    value = value + rim[0] * edge
                elif c >= 6:
                    value = value + rim[c - 5] * north
                right[t, put, :] = value
                value = back_ref[t, put, :]
                if c == 0:
                    inside = jnp.logical_and(wet[0], small < SIDE)
                    value = value + jnp.where(inside, from_s, 0.0)
                elif c == 6:
                    inside = jnp.logical_and(wet[6], small >= 102)
                    value = value + jnp.where(inside, from_n, 0.0)
                elif c == 7:
                    inside = jnp.logical_and(wet[7], small < 4)
                    value = value + jnp.where(inside, from_n, 0.0)
                prev_ref[t, rows, 128 * c : 128 * c + 128] = value
        return carry

    lax.fori_loop(0, GROUPS, rims, 0)
    zero = jnp.zeros((8, 128), F32)
    first = pl.ds(0, 8, stride=8)
    right[0, first, :] = right[0, first, :] + heat_self * tan_t
    right[1, first, :] = right[1, first, :] + salt_heat * tan_t + salt_self * tan_s
    adds = (heat_self * adj_t + salt_heat * adj_s, salt_self * adj_s)
    for t, add in enumerate(adds):
        for c in range(CHUNKS):
            spot = slice(128 * c, 128 * c + 128)
            prev_ref[t, 0:1, spot] = prev_ref[t, 0:1, spot] + add[c : c + 1, :]

    def forward(i, carry):
        y_t, y_s, m = carry
        for s in range(8):
            strided = pl.ds(64 * i + s, 8, stride=8)
            packed = pl.ds(pl.multiple_of(64 * i + 8 * s, 8), 8)
            y_t = right[0, strided, :] + m * y_t
            y_s = right[1, strided, :] + m * y_s
            m = link_ref[packed, :]
            inv = inv_ref[packed, :]
            part[0, packed, :] = y_t * inv
            part[1, packed, :] = y_s * inv
        return y_t, y_s, m

    lax.fori_loop(0, GROUPS, forward, (zero, zero, zero))

    def backward(n, carry):
        x_t, x_s = carry
        i = GROUPS - 1 - n
        for s in reversed(range(8)):
            strided = pl.ds(64 * i + s, 8, stride=8)
            packed = pl.ds(pl.multiple_of(64 * i + 8 * s, 8), 8)
            m = link_ref[packed, :]
            x_t = part[0, packed, :] + m * x_t
            x_s = part[1, packed, :] + m * x_s
            solved[0, strided, :] = x_t
            solved[1, strided, :] = x_s
        return x_t, x_s

    lax.fori_loop(0, GROUPS, backward, (zero, zero))

    def write(i, carry):
        rows = pl.ds(pl.multiple_of(8 * i, 8), 8)
        at = pl.multiple_of(64 * i, 64)
        for t in range(2):
            for c in range(CHUNKS):
                next_ref[t, rows, 128 * c : 128 * c + 128] = solved[
                    t, pl.ds(at + 8 * c, 8), :
                ]
        return carry

    lax.fori_loop(0, GROUPS, write, 0)


def whole(shape):
    return pl.BlockSpec(shape, lambda _: (0,) * len(shape))


def call(kernel, name, outs, in_shapes, out_shapes, scratch=(), scalars=0):
    specs = [pl.BlockSpec(memory_space=pltpu.SMEM)] * scalars
    specs += [whole(shape) for shape in in_shapes]
    return pl.pallas_call(
        kernel,
        grid=(1,),
        in_specs=specs,
        out_specs=[whole(shape) for shape in out_shapes],
        out_shape=[jax.ShapeDtypeStruct(shape, F32) for shape in outs],
        scratch_shapes=list(scratch),
        compiler_params=pltpu.CompilerParams(vmem_limit_bytes=VMEM_LIMIT),
        name=name,
    )


def shift_chips(value, k):
    return lax.ppermute(value, "region", [(i, (i + 2 * k) % 8) for i in range(8)])


def shards(
    tangent, adjoint, base, velocity, kappa, depth_levels, forcing, forcing_point, partner_edge,
    edge_flip,
):
    tangent, adjoint, velocity = tangent[0, 0], adjoint[0, 0], velocity[0, 0]
    base, kappa, depth = base[0, 0], kappa[0, 0], depth_levels[0]
    natural = (2, Z, WIDE)
    blocked = (2, 8 * Z, 128)
    flat = (8 * Z, 128)

    asked = [forcing_point] + [shift_chips(forcing_point, k) for k in (1, 2, 3)]
    banded = forcing.reshape(8, 128, 128).transpose(1, 0, 2).reshape(1024, 128)
    (table,) = call(
        table_kernel, "tables", [(384, 128)], [(1024, 128)], [(384, 128)]
    )(banded)
    mate = lax.ppermute(table, "region", [(i, i ^ 1) for i in range(8)])

    edges, rhs, back, rim, top, link, inv = call(
        main_kernel,
        "main",
        [(136, 128), blocked, blocked, (192, 128), (32, 128), flat, flat],
        [natural, natural, natural, (Z, WIDE), (1, WIDE)],
        [(136, 128), blocked, blocked, (192, 128), (32, 128), flat, flat],
        [
            pltpu.VMEM(flat, F32),
            pltpu.VMEM(blocked, F32),
            pltpu.VMEM(blocked, F32),
            pltpu.VMEM(blocked, F32),
        ],
        scalars=2,
    )(partner_edge[0], edge_flip[0], tangent, adjoint, velocity, kappa, depth)
    near = [edges] + [
        lax.ppermute(edges, "tile", [(i, i ^ k) for i in range(32)]) for k in (1, 2, 3)
    ]

    answers = call(
        lookup_kernel,
        "lookup",
        [(24, 128)] * 4,
        [(384, 128)] * 2 + [(1, 1, CELLS)] * 4,
        [(24, 128)] * 4,
        [pltpu.VMEM((768, 256), jnp.bfloat16), pltpu.VMEM((1, WIDE), jnp.int32)],
    )(table, mate, *asked)
    replies = [answers[0]] + [shift_chips(answers[k], -k) for k in (1, 2, 3)]

    (slots,) = call(
        route_kernel, "route", [(8, 128, 128)], [(136, 128)] * 4, [(8, 128, 128)]
    )(*near)
    groups = [[4 * b + a for b in range(8)] for a in range(4)]
    arrived = lax.all_to_all(slots, "tile", 0, 0, axis_index_groups=groups, tiled=True)

    following, previous = call(
        finish_kernel,
        "finish",
        [(2, Z, CELLS)] * 2,
        [(8, 128, 128), blocked, blocked, (192, 128), (32, 128), flat, flat]
        + [(24, 128)] * 4
        + [(1, WIDE), (2, WIDE)],
        [natural, natural],
        [
            pltpu.VMEM(blocked, F32),
            pltpu.VMEM(blocked, F32),
            pltpu.VMEM(blocked, F32),
            pltpu.VMEM((3, 8, 128), F32),
        ],
    )(arrived, rhs, back, rim, top, link, inv, *replies, depth, base)
    return following[None, None], previous[None, None]


def solution(mesh):
    fields = P("region", "tile", None, None, None)
    rows = P("region", "tile", None, None)
    single = P("region", "tile", None)
    in_specs = (fields, fields, rows, fields, rows, single, P(None, "region"), single, single, single)
    return jax.shard_map(
        shards, mesh=mesh, in_specs=in_specs, out_specs=(fields, fields), check_vma=False
    )
```

```python
import jax
import jax.numpy as jnp
from jax import lax
from jax.experimental import pallas as pl
from jax.experimental.pallas import tpu as pltpu
from jax.sharding import PartitionSpec as P

SIDE = 30
Z = 64
CELLS = SIDE * SIDE
WIDE = 1024
CHUNKS = WIDE // 128
GROUPS = Z // 8
D = 0.2
CENTRE = 1.0 - 4.0 * D
F32 = jnp.float32
SOLVE_LIMIT = 54 * 1024 * 1024
VMEM_LIMIT = 8 * 1024 * 1024


def lanes(rows, width=WIDE):
    return lax.broadcasted_iota(jnp.int32, (rows, width), 1)


def split(row):
    return [row[:, 128 * c : 128 * c + 128] for c in range(CHUNKS)]


def roll(value, shift):
    return pltpu.roll(value, shift % value.shape[-1], value.ndim - 1)


def grid_masks(rows=1):
    cell = lanes(rows)
    y = lax.shift_right_logical(cell * 2185, 16)
    x = cell - y * SIDE
    return x == 0, x == SIDE - 1, y == 0, y == SIDE - 1


def mirrored(value):
    lane = lanes(value.shape[0], 128)
    back = jnp.bitwise_and(131 - lane, 127)
    turned = [jnp.take_along_axis(part, back, axis=1) for part in split(value)]
    return jnp.concatenate(
        [
            jnp.where(lane < 4, turned[7 - c], turned[max(6 - c, 0)])
            for c in range(CHUNKS)
        ],
        axis=1,
    )


def pieces_of(ref, *at):
    tail = ref[(*at, slice(WIDE - 128, CELLS))]
    fill = jnp.zeros(tail.shape[:-1] + (WIDE - CELLS,), tail.dtype)
    full = [ref[(*at, slice(128 * c, 128 * c + 128))] for c in range(CHUNKS - 1)]
    return full + [jnp.concatenate([tail, fill], axis=-1)]


def put_piece(ref, t, rows, c, value):
    if c < CHUNKS - 1:
        ref[t, rows, 128 * c : 128 * c + 128] = value
    else:
        ref[t, rows, 128 * c : CELLS] = value[:, 0 : CELLS - 128 * c]


def wide(ref, *at):
    return jnp.concatenate(pieces_of(ref, *at), axis=-1)


def make_table(forcing_ref, table_ref):
    wu, wv, ta, qa, pr, ro, ps, ic = [
        forcing_ref[pl.ds(field, 128, stride=8), :] for field in range(8)
    ]
    speed = jnp.sqrt(wu * wu + wv * wv + 1.0)
    carrier = jnp.exp(0.3 * (ps - ta)) * speed / (1.0 + jnp.exp(ic))
    table_ref[0:128, :] = carrier
    table_ref[128:256, :] = carrier * jnp.exp(-0.2 * ps)
    table_ref[256:384, :] = 0.5 * carrier * qa + pr + ro


def lookup_kernel(own_ref, mate_ref, q0, q1, q2, q3, a0, a1, a2, a3, pieces):
    band = lax.axis_index("region")
    for number, ref in enumerate((own_ref, mate_ref)):
        value = ref[...]
        coarse = value.astype(jnp.bfloat16)
        pieces[384 * number : 384 * number + 384, 0:128] = coarse
        pieces[384 * number : 384 * number + 384, 128:256] = (
            value - coarse.astype(F32)
        ).astype(jnp.bfloat16)
    base_own = band * 128
    base_mate = (band + 1 - 2 * lax.rem(band, 2)) * 128
    low = jnp.bitwise_and(lax.broadcasted_iota(jnp.int32, (256, 256), 0), 127)
    high = lax.broadcasted_iota(jnp.int32, (128, 256), 0)
    for q_ref, a_ref in ((q0, a0), (q1, a1), (q2, a2), (q3, a3)):
        points = pieces_of(q_ref, slice(0, 1))
        for part in range(4):
            point = jnp.concatenate(points[2 * part : 2 * part + 2], axis=1)
            onehot = (low == jnp.bitwise_and(point, 127)).astype(jnp.bfloat16)
            found = jnp.dot(pieces[...], onehot, preferred_element_type=F32)
            row = lax.shift_right_logical(point, 7)
            here = high == row - base_own
            there = high == row - base_mate
            for field in range(3):
                picked = jnp.where(here, found[128 * field : 128 * field + 128], 0.0)
                picked = picked + jnp.where(
                    there, found[384 + 128 * field : 512 + 128 * field], 0.0
                )
                total = jnp.sum(picked, axis=0, keepdims=True)
                at = 8 * field + 2 * part
                a_ref[at : at + 1, :] = total[:, 0:128]
                a_ref[at + 1 : at + 2, :] = total[:, 128:256]


def solve_kernel(
    partner_ref, flip_ref, adj_hbm, kap_hbm, depth_hbm, vel_hbm, tan_hbm, forcing_hbm,
    edge_ref, depth_ref, table_ref, solved_hbm, peak_ref, link_ref,
    coup, given, part, solved, adj_ref, kap_ref, forcing_ref, vel_ref, tan_ref, done,
):
    copies = [
        pltpu.make_async_copy(source, target, done.at[number])
        for number, (source, target) in enumerate(
            (
                (kap_hbm, kap_ref),
                (depth_hbm, depth_ref),
                (adj_hbm, adj_ref),
                (forcing_hbm, forcing_ref),
                (vel_hbm, vel_ref),
                (tan_hbm, tan_ref),
            )
        )
    ]
    for copy in copies:
        copy.start()
    copies[0].wait()
    copies[1].wait()
    depths = pieces_of(depth_ref, slice(0, 1))
    for level in range(Z - 1):
        for c, piece in enumerate(pieces_of(kap_ref, level, slice(0, 1))):
            coup[8 * level + c : 8 * level + c + 1, :] = piece
    coup[8 * Z - 8 :, :] = jnp.zeros((8, 128), F32)
    for c, piece in enumerate(depths):
        peak_ref[c : c + 1, :] = piece.astype(F32)
    columns = peak_ref[0:8, :].astype(jnp.int32)

    copies[2].wait()

    def relayout(i, carry):
        rows = pl.ds(pl.multiple_of(8 * i, 8), 8)
        at = pl.multiple_of(64 * i, 64)
        for t in range(2):
            for c, piece in enumerate(pieces_of(adj_ref, t, rows)):
                given[t, pl.ds(at + 8 * c, 8), :] = piece
        return carry

    lax.fori_loop(0, GROUPS, relayout, 0)

    def forward(i, carry):
        e, y_t, y_s, m = carry
        for s in range(8):
            strided = pl.ds(64 * i + s, 8, stride=8)
            packed = pl.ds(pl.multiple_of(64 * i + 8 * s, 8), 8)
            link = jnp.where(8 * i + s + 1 < columns, coup[packed, :], 0.0)
            inv = 1.0 / (e + link)
            y_t = given[0, strided, :] + m * y_t
            y_s = given[1, strided, :] + m * y_s
            m = link * inv
            e = 1.0 + m * e
            link_ref[pl.ds(pl.multiple_of(512 + 64 * i + 8 * s, 8), 8), :] = inv
            link_ref[packed, :] = m
            part[0, packed, :] = y_t * inv
            part[1, packed, :] = y_s * inv
        return e, y_t, y_s, m

    zero = jnp.zeros((8, 128), F32)
    lax.fori_loop(0, GROUPS, forward, (zero + 1.0, zero, zero, zero))

    def backward(n, carry):
        x_t, x_s = carry
        i = GROUPS - 1 - n
        for s in reversed(range(8)):
            strided = pl.ds(64 * i + s, 8, stride=8)
            packed = pl.ds(pl.multiple_of(64 * i + 8 * s, 8), 8)
            m = link_ref[packed, :]
            x_t = part[0, packed, :] + m * x_t
            x_s = part[1, packed, :] + m * x_s
            solved[0, strided, :] = x_t
            solved[1, strided, :] = x_s
        return x_t, x_s

    x_t, x_s = lax.fori_loop(0, GROUPS, backward, (zero, zero))
    peak_ref[0:8, :] = x_t
    peak_ref[8:16, :] = x_s
    keep = pltpu.make_async_copy(solved, solved_hbm, done.at[6])
    keep.start()
    copies[3].wait()
    make_table(forcing_ref, table_ref)
    for copy in copies[4:]:
        copy.wait()

    small = lanes(8, 128)
    south, north = flip_ref[0, 2] == 1, flip_ref[0, 3] == 1
    order = small
    for first, turn in ((0, south), (30, north), (60, south), (90, north)):
        inside = jnp.logical_and(small >= first, small < first + SIDE)
        order = jnp.where(
            jnp.logical_and(inside, turn), 2 * first + SIDE - 1 - small, order
        )
    upper = small >= 102
    level = lax.broadcasted_iota(jnp.int32, (8, 128), 0)

    def pack(i, carry):
        rows = pl.ds(pl.multiple_of(8 * i, 8), 8)
        at = pl.multiple_of(64 * i, 64)
        wet = {c: level + 8 * i < depths[c] for c in (0, 6, 7)}
        speed = pieces_of(vel_ref, 1, rows)
        half = {c: 0.5 * speed[c] for c in (0, 6, 7)}
        for t in range(2):
            value, push = {}, {}
            tracer = pieces_of(tan_ref, t, rows)
            for c in (0, 6, 7):
                value[c] = jnp.where(wet[c], tracer[c], 0.0)
                factor = D + half[c] if c == 0 else D - half[c]
                push[c] = jnp.where(
                    wet[c], factor * solved[t, pl.ds(at + 8 * c, 8), :], 0.0
                )
            edges = jnp.where(small < 30, value[0], 0.0)
            packs = (
                (roll(jnp.where(upper, value[6], value[7]), 56), 30),
                (roll(push[0], 60), 60),
                (roll(jnp.where(upper, push[6], push[7]), 116), 90),
            )
            for piece, first in packs:
                inside = jnp.logical_and(small >= first, small < first + SIDE)
                edges = jnp.where(inside, piece, edges)
            edges = jnp.take_along_axis(edges, order, axis=1)
            edge_ref[pl.ds(pl.multiple_of(64 * t + 8 * i, 8), 8), :] = edges
        return carry

    lax.fori_loop(0, GROUPS, pack, 0, unroll=4)
    second = jnp.logical_or(small < 30, jnp.logical_and(small >= 60, small < 90))
    target = jnp.where(
        second,
        lax.shift_right_logical(partner_ref[0, 2], 2),
        lax.shift_right_logical(partner_ref[0, 3], 2),
    )
    edge_ref[128:136, :] = jnp.where(small < 120, target, -1).astype(F32)
    keep.wait()


def stencil_kernel(
    flip_ref, tan_ref, vel_ref, depth_ref, base_ref, solved, rhs_ref, back_ref, rim_ref,
):
    depth = wide(depth_ref, slice(0, 1))
    sub = lax.broadcasted_iota(jnp.int32, (8, WIDE), 0)
    x0, x29, y0, y29 = grid_masks(8)
    ends = jnp.logical_or(x29, lanes(8) == WIDE - 1)
    turned = jnp.full((8, WIDE), flip_ref[0, 0] == 1)
    turned_x0 = jnp.logical_and(turned, x0)
    turned_x29 = jnp.logical_and(turned, x29)
    small = lanes(8, 128)

    def stencil(i, carry):
        rows = pl.ds(pl.multiple_of(8 * i, 8), 8)
        at = pl.multiple_of(64 * i, 64)
        wet = sub + 8 * i < depth
        half_x, half_y = 0.5 * wide(vel_ref, 0, rows), 0.5 * wide(vel_ref, 1, rows)
        to_e, to_w, to_n, to_s = D - half_x, D + half_x, D - half_y, D + half_y
        for t in range(2):
            value = jnp.where(wet, wide(tan_ref, t, rows), 0.0)
            image = mirrored(value)
            above, below = roll(value, -SIDE), roll(value, SIDE)
            east = roll(jnp.where(x0, below, value), -1)
            west = roll(jnp.where(ends, above, value), 1)
            east = jnp.where(turned_x29, image, east)
            west = jnp.where(turned_x0, image, west)
            mixed = CENTRE * value + to_e * east + to_w * west
            mixed = mixed + to_n * jnp.where(y29, 0.0, above)
            mixed = mixed + to_s * jnp.where(y0, 0.0, below)
            mixed = jnp.where(wet, mixed, 0.0)
            for c, piece in enumerate(split(mixed)):
                rhs_ref[t, pl.ds(at + 8 * c, 8), :] = piece

            answer = jnp.concatenate(
                [solved[t, pl.ds(at + 8 * c, 8), :] for c in range(CHUNKS)], axis=1
            )
            answer = jnp.where(wet, answer, 0.0)
            push_e, push_w = to_e * answer, to_w * answer
            image = mirrored(jnp.where(x29, push_e, push_w))
            moved_e, moved_w = roll(push_e, 1), roll(push_w, -1)
            straight_e = jnp.where(turned_x0, image, jnp.where(x0, 0.0, moved_e))
            straight_w = jnp.where(turned_x29, image, jnp.where(x29, 0.0, moved_w))
            cross_e = jnp.where(x0, jnp.where(turned, 0.0, moved_e), 0.0)
            cross_w = jnp.where(ends, jnp.where(turned, 0.0, moved_w), 0.0)
            inner = CENTRE * answer + straight_e + straight_w
            inner = inner + roll(to_n * answer + cross_w, SIDE)
            inner = inner + roll(to_s * answer + cross_e, -SIDE)
            inner = jnp.where(wet, inner, 0.0)
            for c, piece in enumerate(split(inner)):
                put_piece(back_ref, t, rows, c, piece)
        wet, to_n, to_s = split(wet), split(to_n), split(to_s)
        rim = (
            jnp.where(jnp.logical_and(wet[0], small < SIDE), to_s[0], 0.0),
            jnp.where(jnp.logical_and(wet[6], small >= 102), to_n[6], 0.0),
            jnp.where(jnp.logical_and(wet[7], small < 4), to_n[7], 0.0),
        )
        for number, piece in enumerate(rim):
            rim_ref[pl.ds(pl.multiple_of(64 * number + 8 * i, 8), 8), :] = piece
        return carry

    lax.fori_loop(0, GROUPS, stencil, 0)
    wet = 0 < depth
    for t in range(2):
        first = wide(tan_ref, t, slice(0, 1))
        for c, piece in enumerate(split(jnp.where(wet, first, 0.0))):
            rim_ref[192 + 8 * t + c : 193 + 8 * t + c, :] = piece
        for c, piece in enumerate(pieces_of(base_ref, slice(t, t + 1))):
            rim_ref[208 + 8 * t + c : 209 + 8 * t + c, :] = piece
    for c, piece in enumerate(split(depth)):
        rim_ref[224 + c : 225 + c, :] = piece.astype(F32)


def route_kernel(e0, e1, e2, e3, out_ref):
    mine = lax.shift_right_logical(lax.axis_index("tile"), 3)
    sources = (e0, e1, e2, e3)
    goals = [ref[128:129, :].astype(jnp.int32) for ref in sources]
    for b in range(8):
        total = jnp.zeros((128, 128), F32)
        for goal, ref in zip(goals, sources):
            total = jnp.where(goal == 8 * mine + b, ref[0:128, :], total)
        out_ref[b] = total


def finish_kernel(
    edge_ref, rhs_ref, back_hbm, rim_ref, peak_ref, link_ref,
    r0, r1, r2, r3, depth_ref, next_hbm, prev_hbm,
    right, part, solved, next_ref, prev_ref, done,
):
    fetch = pltpu.make_async_copy(back_hbm, prev_ref, done.at[2])
    fetch.start()
    depth = wide(depth_ref, slice(0, 1))
    carrier, scaled, loss = [
        sum(ref[8 * f : 8 * f + 8, :] for ref in (r0, r1, r2, r3)) for f in range(3)
    ]
    moist = scaled * jnp.exp(0.5 * rim_ref[208:216, :])
    wet = rim_ref[224:232, :] > 0.0
    heat_self = jnp.where(wet, -(0.5 * carrier + 0.25 * moist), 0.0)
    salt_heat = jnp.where(wet, 0.25 * rim_ref[216:224, :] * moist, 0.0)
    salt_self = jnp.where(wet, 0.5 * moist - loss, 0.0)
    tan_t, tan_s = rim_ref[192:200, :], rim_ref[200:208, :]
    adj_t, adj_s = peak_ref[0:8, :], peak_ref[8:16, :]

    small = lanes(8, 128)
    sub = lax.broadcasted_iota(jnp.int32, (8, WIDE), 0)

    def rims(i, carry):
        rows = pl.ds(pl.multiple_of(8 * i, 8), 8)
        at = pl.multiple_of(64 * i, 64)
        wet = split(sub + 8 * i < depth)
        rim = [rim_ref[pl.ds(pl.multiple_of(64 * n + 8 * i, 8), 8), :] for n in range(3)]
        for t in range(2):
            where = pl.ds(pl.multiple_of(64 * t + 8 * i, 8), 8)
            edge = edge_ref[0, where, :]
            for b in range(1, 8):
                edge = edge + edge_ref[b, where, :]
            north = roll(edge, 72)
            from_s, from_n = roll(edge, 68), roll(edge, 12)
            for c in range(CHUNKS):
                put = pl.ds(at + 8 * c, 8)
                value = rhs_ref[t, put, :]
                if c == 0:
                    value = value + rim[0] * edge
                elif c >= 6:
                    value = value + rim[c - 5] * north
                right[t, put, :] = value
            insides = (
                (0, jnp.logical_and(wet[0], small < SIDE), from_s),
                (6, jnp.logical_and(wet[6], small >= 102), from_n),
                (7, jnp.logical_and(wet[7], small < 4), from_n),
            )
            for c, inside, piece in insides:
                spot = slice(128 * c, min(128 * c + 128, CELLS))
                piece = jnp.where(inside, piece, 0.0)[:, 0 : spot.stop - spot.start]
                prev_ref[t, rows, spot] = prev_ref[t, rows, spot] + piece
        return carry

    fetch.wait()
    lax.fori_loop(0, GROUPS, rims, 0)
    zero = jnp.zeros((8, 128), F32)
    first = pl.ds(0, 8, stride=8)
    right[0, first, :] = right[0, first, :] + heat_self * tan_t
    right[1, first, :] = right[1, first, :] + salt_heat * tan_t + salt_self * tan_s
    adds = (heat_self * adj_t + salt_heat * adj_s, salt_self * adj_s)
    for t, add in enumerate(adds):
        for c in range(CHUNKS):
            spot = slice(128 * c, min(128 * c + 128, CELLS))
            more = add[c : c + 1, 0 : spot.stop - spot.start]
            prev_ref[t, 0:1, spot] = prev_ref[t, 0:1, spot] + more
    copy_prev = pltpu.make_async_copy(prev_ref, prev_hbm, done.at[0])
    copy_prev.start()

    def forward(i, carry):
        y_t, y_s, m = carry
        for s in range(8):
            strided = pl.ds(64 * i + s, 8, stride=8)
            packed = pl.ds(pl.multiple_of(64 * i + 8 * s, 8), 8)
            y_t = right[0, strided, :] + m * y_t
            y_s = right[1, strided, :] + m * y_s
            m = link_ref[packed, :]
            inv = link_ref[pl.ds(pl.multiple_of(512 + 64 * i + 8 * s, 8), 8), :]
            part[0, packed, :] = y_t * inv
            part[1, packed, :] = y_s * inv
        return y_t, y_s, m

    lax.fori_loop(0, GROUPS, forward, (zero, zero, zero))

    def backward(n, carry):
        x_t, x_s = carry
        i = GROUPS - 1 - n
        for s in reversed(range(8)):
            strided = pl.ds(64 * i + s, 8, stride=8)
            packed = pl.ds(pl.multiple_of(64 * i + 8 * s, 8), 8)
            m = link_ref[packed, :]
            x_t = part[0, packed, :] + m * x_t
            x_s = part[1, packed, :] + m * x_s
            solved[0, strided, :] = x_t
            solved[1, strided, :] = x_s
        return x_t, x_s

    lax.fori_loop(0, GROUPS, backward, (zero, zero))

    def write(i, carry):
        rows = pl.ds(pl.multiple_of(8 * i, 8), 8)
        at = pl.multiple_of(64 * i, 64)
        for t in range(2):
            for c in range(CHUNKS):
                put_piece(next_ref, t, rows, c, solved[t, pl.ds(at + 8 * c, 8), :])
        return carry

    lax.fori_loop(0, GROUPS, write, 0)
    copy_next = pltpu.make_async_copy(next_ref, next_hbm, done.at[1])
    copy_next.start()
    copy_next.wait()
    copy_prev.wait()


def call(kernel, name, micros, ins, outs, scratch=(), limit=VMEM_LIMIT):
    places = {"S": pltpu.SMEM, "V": pltpu.VMEM, "H": pltpu.HBM}
    shapes = [
        out if isinstance(out, jax.ShapeDtypeStruct) else jax.ShapeDtypeStruct(out, F32)
        for _, out in outs
    ]
    return pl.pallas_call(
        kernel,
        in_specs=[pl.BlockSpec(memory_space=places[place]) for place in ins],
        out_specs=[pl.BlockSpec(memory_space=places[place]) for place, _ in outs],
        out_shape=shapes,
        scratch_shapes=list(scratch),
        compiler_params=pltpu.CompilerParams(vmem_limit_bytes=limit),
        cost_estimate=pl.CostEstimate(
            flops=0, bytes_accessed=int(3.69e6 * micros), transcendentals=0
        ),
        name=name,
    )


def swap(value, axis, size, bit):
    return lax.ppermute(value, axis, [(i, i ^ bit) for i in range(size)])


def hops():
    ways = ([], [], [])
    for h in range(4):
        for low in range(2):
            step = 2 * low - 1
            targets = (((h + step) % 4, 1 - low), ((h - step) % 4, low), ((h + 2) % 4, 1 - low))
            for way, (there, low_there) in zip(ways, targets):
                for core in range(2):
                    for column in range(16):
                        source = (2 * h + core) * 32 + 2 * column + low
                        target = (2 * there + core) * 32 + 2 * column + low_there
                        way.append((source, target))
    return ways


def shards(
    tangent, adjoint, base, velocity, kappa, depth_levels, forcing, forcing_point, partner_edge,
    edge_flip,
):
    tangent, adjoint, velocity = tangent[0, 0], adjoint[0, 0], velocity[0, 0]
    base, kappa, depth = base[0, 0], kappa.reshape(Z - 1, 1, CELLS), depth_levels[0]
    mine, partner, flip = forcing_point[0], partner_edge[0], edge_flip[0]
    blocked = (2, 8 * Z, 128)
    flat = (8 * Z, 128)
    natural = (2, Z, CELLS)
    answer = (24, 128)
    line = jax.ShapeDtypeStruct((1, CELLS), jnp.int32)
    both = ("region", "tile")

    asked = [lax.ppermute(mine, both, way) for way in hops()]
    banded = forcing.reshape(8, 128, 128).transpose(1, 0, 2).reshape(1024, 128)
    edges, depth, table, solved, peak, link = call(
        solve_kernel,
        "solve",
        4.0,
        "SSHHHHHH",
        [("V", (136, 128)), ("V", line), ("V", (384, 128))]
        + [("H", blocked), ("V", (16, 128)), ("V", (16 * Z, 128))],
        [
            pltpu.VMEM(flat, F32),
            pltpu.VMEM(blocked, F32),
            pltpu.VMEM(blocked, F32),
            pltpu.VMEM(blocked, F32),
            pltpu.VMEM(natural, F32),
            pltpu.VMEM((Z - 1, 1, CELLS), F32),
            pltpu.VMEM((1024, 128), F32),
            pltpu.VMEM(natural, F32),
            pltpu.VMEM(natural, F32),
            pltpu.SemaphoreType.DMA((7,)),
        ],
        limit=SOLVE_LIMIT,
    )(partner, flip, adjoint, kappa, depth, velocity, tangent, banded)
    table, edges, asked = lax.optimization_barrier((table, edges, asked))
    mate = swap(table, "region", 8, 1)
    edge = [edges] + [swap(edges, "tile", 32, k) for k in (8, 16, 24)]

    table, edges = lax.optimization_barrier((table, edges))
    answers = call(
        lookup_kernel,
        "lookup",
        2.7,
        "V" * 6,
        [("V", answer)] * 4,
        [pltpu.VMEM((768, 256), jnp.bfloat16)],
    )(table, mate, mine, *asked)
    replies = [answers[0]] + [
        lax.ppermute(value, both, [(target, source) for source, target in way])
        for value, way in zip(answers[1:], hops())
    ]

    edge[0], first = lax.optimization_barrier((edge[0], answers[0]))
    (slots,) = call(route_kernel, "route", 0.9, "VVVV", [("V", (8, 128, 128))])(*edge)
    groups = [[8 * a + b for b in range(8)] for a in range(4)]
    arrived = lax.all_to_all(slots, "tile", 0, 0, axis_index_groups=groups, tiled=True)

    rhs, back, rim = call(
        stencil_kernel,
        "stencil",
        3.0,
        "SVVVVV",
        [("V", blocked), ("V", natural), ("V", (232, 128))],
    )(flip, tangent, velocity, depth, base, solved)

    following, previous = call(
        finish_kernel,
        "finish",
        2.1,
        "VVHVVVVVVVV",
        [("H", natural), ("H", natural)],
        [
            pltpu.VMEM(blocked, F32),
            pltpu.VMEM(blocked, F32),
            pltpu.VMEM(blocked, F32),
            pltpu.VMEM(natural, F32),
            pltpu.VMEM(natural, F32),
            pltpu.SemaphoreType.DMA((3,)),
        ],
    )(arrived, rhs, back, rim, peak, link, *replies, depth)
    return following[None, None], previous[None, None]


def solution(mesh):
    fields = P("region", "tile", None, None, None)
    rows = P("region", "tile", None, None)
    single = P("region", "tile", None)
    in_specs = (fields, fields, rows, fields, rows, single, P(None, "region"), single, single, single)
    return jax.shard_map(
        shards, mesh=mesh, in_specs=in_specs, out_specs=(fields, fields), check_vma=False
    )
```

```python
import jax
import jax.numpy as jnp
from jax import lax
from jax.experimental import pallas as pl
from jax.experimental.pallas import tpu as pltpu
from jax.sharding import PartitionSpec as P

SIDE = 30
Z = 64
CELLS = SIDE * SIDE
WIDE = 1024
CHUNKS = WIDE // 128
GROUPS = Z // 8
D = 0.2
CENTRE = 1.0 - 4.0 * D
F32 = jnp.float32
SOLVE_LIMIT = 53 * 1024 * 1024 + 512 * 1024
VMEM_LIMIT = 8 * 1024 * 1024


def lanes(rows, width=WIDE):
    return lax.broadcasted_iota(jnp.int32, (rows, width), 1)


def split(row):
    return [row[:, 128 * c : 128 * c + 128] for c in range(CHUNKS)]


def roll(value, shift):
    return pltpu.roll(value, shift % value.shape[-1], value.ndim - 1)


def grid_masks(rows=1):
    cell = lanes(rows)
    y = lax.shift_right_logical(cell * 2185, 16)
    x = cell - y * SIDE
    return x == 0, x == SIDE - 1, y == 0, y == SIDE - 1


def mirrored(value):
    lane = lanes(value.shape[0], 128)
    back = jnp.bitwise_and(131 - lane, 127)
    turned = [jnp.take_along_axis(part, back, axis=1) for part in split(value)]
    return jnp.concatenate(
        [
            jnp.where(lane < 4, turned[7 - c], turned[max(6 - c, 0)])
            for c in range(CHUNKS)
        ],
        axis=1,
    )


def pieces_of(ref, *at):
    tail = ref[(*at, slice(WIDE - 128, CELLS))]
    fill = jnp.zeros(tail.shape[:-1] + (WIDE - CELLS,), tail.dtype)
    full = [ref[(*at, slice(128 * c, 128 * c + 128))] for c in range(CHUNKS - 1)]
    return full + [jnp.concatenate([tail, fill], axis=-1)]


def put_piece(ref, t, rows, c, value):
    if c < CHUNKS - 1:
        ref[t, rows, 128 * c : 128 * c + 128] = value
    else:
        ref[t, rows, 128 * c : CELLS] = value[:, 0 : CELLS - 128 * c]


def wide(ref, *at):
    return jnp.concatenate(pieces_of(ref, *at), axis=-1)


def make_table(forcing_ref, table_ref):
    wu, wv, ta, qa, pr, ro, ps, ic = [
        forcing_ref[pl.ds(field, 128, stride=8), :] for field in range(8)
    ]
    speed = jnp.sqrt(wu * wu + wv * wv + 1.0)
    carrier = jnp.exp(0.3 * (ps - ta)) * speed / (1.0 + jnp.exp(ic))
    table_ref[0:128, :] = carrier
    table_ref[128:256, :] = carrier * jnp.exp(-0.2 * ps)
    table_ref[256:384, :] = 0.5 * carrier * qa + pr + ro


def lookup_kernel(own_ref, mate_ref, q0, q1, q2, q3, a0, a1, a2, a3, pieces):
    band = lax.axis_index("region")
    for number, ref in enumerate((own_ref, mate_ref)):
        value = ref[...]
        coarse = value.astype(jnp.bfloat16)
        pieces[384 * number : 384 * number + 384, 0:128] = coarse
        pieces[384 * number : 384 * number + 384, 128:256] = (
            value - coarse.astype(F32)
        ).astype(jnp.bfloat16)
    base_own = band * 128
    base_mate = (band + 1 - 2 * lax.rem(band, 2)) * 128
    low = jnp.bitwise_and(lax.broadcasted_iota(jnp.int32, (256, 256), 0), 127)
    high = lax.broadcasted_iota(jnp.int32, (128, 256), 0)
    for q_ref, a_ref in ((q0, a0), (q1, a1), (q2, a2), (q3, a3)):
        points = pieces_of(q_ref, slice(0, 1))
        for part in range(4):
            point = jnp.concatenate(points[2 * part : 2 * part + 2], axis=1)
            onehot = (low == jnp.bitwise_and(point, 127)).astype(jnp.bfloat16)
            found = jnp.dot(pieces[...], onehot, preferred_element_type=F32)
            row = lax.shift_right_logical(point, 7)
            here = high == row - base_own
            there = high == row - base_mate
            for field in range(3):
                picked = jnp.where(here, found[128 * field : 128 * field + 128], 0.0)
                picked = picked + jnp.where(
                    there, found[384 + 128 * field : 512 + 128 * field], 0.0
                )
                total = jnp.sum(picked, axis=0, keepdims=True)
                at = 8 * field + 2 * part
                a_ref[at : at + 1, :] = total[:, 0:128]
                a_ref[at + 1 : at + 2, :] = total[:, 128:256]


def solve_kernel(
    partner_ref, flip_ref, adj_hbm, kap_hbm, depth_hbm, vel_hbm, tan_hbm, forcing_hbm, base_hbm,
    edge_ref, depth_ref, table_ref, solved_hbm, peak_ref, link_hbm,
    coup, given, part, solved, link_ref, adj_ref, kap_ref, forcing_ref, vel_ref, tan_ref, base_ref, done,
):
    copies = [
        pltpu.make_async_copy(source, target, done.at[number])
        for number, (source, target) in enumerate(
            (
                (kap_hbm, kap_ref),
                (depth_hbm, depth_ref),
                (adj_hbm, adj_ref),
                (forcing_hbm, forcing_ref),
                (vel_hbm, vel_ref),
                (tan_hbm, tan_ref),
                (base_hbm, base_ref),
            )
        )
    ]
    for copy in copies:
        copy.start()
    copies[0].wait()
    copies[1].wait()
    depths = pieces_of(depth_ref, slice(0, 1))
    for level in range(Z - 1):
        for c, piece in enumerate(pieces_of(kap_ref, level, slice(0, 1))):
            coup[8 * level + c : 8 * level + c + 1, :] = piece
    coup[8 * Z - 8 :, :] = jnp.zeros((8, 128), F32)
    for c, piece in enumerate(depths):
        peak_ref[c : c + 1, :] = piece.astype(F32)
    columns = peak_ref[0:8, :].astype(jnp.int32)

    copies[2].wait()

    def relayout(i, carry):
        rows = pl.ds(pl.multiple_of(8 * i, 8), 8)
        at = pl.multiple_of(64 * i, 64)
        for t in range(2):
            for c, piece in enumerate(pieces_of(adj_ref, t, rows)):
                given[t, pl.ds(at + 8 * c, 8), :] = piece
        return carry

    lax.fori_loop(0, GROUPS, relayout, 0)

    def forward(i, carry):
        e, y_t, y_s, m = carry
        for s in range(8):
            strided = pl.ds(64 * i + s, 8, stride=8)
            packed = pl.ds(pl.multiple_of(64 * i + 8 * s, 8), 8)
            link = jnp.where(8 * i + s + 1 < columns, coup[packed, :], 0.0)
            inv = 1.0 / (e + link)
            y_t = given[0, strided, :] + m * y_t
            y_s = given[1, strided, :] + m * y_s
            m = link * inv
            e = 1.0 + m * e
            link_ref[pl.ds(pl.multiple_of(512 + 64 * i + 8 * s, 8), 8), :] = inv
            link_ref[packed, :] = m
            part[0, packed, :] = y_t * inv
            part[1, packed, :] = y_s * inv
        return e, y_t, y_s, m

    zero = jnp.zeros((8, 128), F32)
    lax.fori_loop(0, GROUPS, forward, (zero + 1.0, zero, zero, zero))
    keep_link = pltpu.make_async_copy(link_ref, link_hbm, done.at[8])
    keep_link.start()

    def backward(n, carry):
        x_t, x_s = carry
        i = GROUPS - 1 - n
        for s in reversed(range(8)):
            strided = pl.ds(64 * i + s, 8, stride=8)
            packed = pl.ds(pl.multiple_of(64 * i + 8 * s, 8), 8)
            m = link_ref[packed, :]
            x_t = part[0, packed, :] + m * x_t
            x_s = part[1, packed, :] + m * x_s
            solved[0, strided, :] = x_t
            solved[1, strided, :] = x_s
        return x_t, x_s

    x_t, x_s = lax.fori_loop(0, GROUPS, backward, (zero, zero))
    peak_ref[0:8, :] = x_t
    peak_ref[8:16, :] = x_s
    keep = pltpu.make_async_copy(solved, solved_hbm, done.at[7])
    keep.start()
    copies[3].wait()
    make_table(forcing_ref, table_ref)
    for copy in copies[4:]:
        copy.wait()
    for t in range(2):
        for c, piece in enumerate(pieces_of(base_ref, slice(t, t + 1))):
            peak_ref[16 + 8 * t + c : 17 + 8 * t + c, :] = piece
        for c, piece in enumerate(pieces_of(tan_ref, t, slice(0, 1))):
            wet = depths[c] > 0
            peak_ref[32 + 8 * t + c : 33 + 8 * t + c, :] = jnp.where(wet, piece, 0.0)
    for c, piece in enumerate(depths):
        peak_ref[48 + c : 49 + c, :] = piece.astype(F32)

    small = lanes(8, 128)
    south, north = flip_ref[0, 2] == 1, flip_ref[0, 3] == 1
    order = small
    for first, turn in ((0, south), (30, north), (60, south), (90, north)):
        inside = jnp.logical_and(small >= first, small < first + SIDE)
        order = jnp.where(
            jnp.logical_and(inside, turn), 2 * first + SIDE - 1 - small, order
        )
    upper = small >= 102
    level = lax.broadcasted_iota(jnp.int32, (8, 128), 0)

    def pack(i, carry):
        rows = pl.ds(pl.multiple_of(8 * i, 8), 8)
        at = pl.multiple_of(64 * i, 64)
        wet = {c: level + 8 * i < depths[c] for c in (0, 6, 7)}
        speed = pieces_of(vel_ref, 1, rows)
        half = {c: 0.5 * speed[c] for c in (0, 6, 7)}
        for t in range(2):
            value, push = {}, {}
            tracer = pieces_of(tan_ref, t, rows)
            for c in (0, 6, 7):
                value[c] = jnp.where(wet[c], tracer[c], 0.0)
                factor = D + half[c] if c == 0 else D - half[c]
                push[c] = jnp.where(
                    wet[c], factor * solved[t, pl.ds(at + 8 * c, 8), :], 0.0
                )
            edges = jnp.where(small < 30, value[0], 0.0)
            packs = (
                (roll(jnp.where(upper, value[6], value[7]), 56), 30),
                (roll(push[0], 60), 60),
                (roll(jnp.where(upper, push[6], push[7]), 116), 90),
            )
            for piece, first in packs:
                inside = jnp.logical_and(small >= first, small < first + SIDE)
                edges = jnp.where(inside, piece, edges)
            edges = jnp.take_along_axis(edges, order, axis=1)
            edge_ref[pl.ds(pl.multiple_of(64 * t + 8 * i, 8), 8), :] = edges
        return carry

    lax.fori_loop(0, GROUPS, pack, 0, unroll=4)
    second = jnp.logical_or(small < 30, jnp.logical_and(small >= 60, small < 90))
    target = jnp.where(
        second,
        lax.shift_right_logical(partner_ref[0, 2], 2),
        lax.shift_right_logical(partner_ref[0, 3], 2),
    )
    edge_ref[128:136, :] = jnp.where(small < 120, target, -1).astype(F32)
    keep.wait()
    keep_link.wait()


def stencil_kernel(
    flip_ref, tan_ref, vel_ref, depth_ref, solved, rhs_ref, back_ref, rim_ref,
):
    depth = wide(depth_ref, slice(0, 1))
    sub = lax.broadcasted_iota(jnp.int32, (8, WIDE), 0)
    x0, x29, y0, y29 = grid_masks(8)
    ends = jnp.logical_or(x29, lanes(8) == WIDE - 1)
    turned = jnp.full((8, WIDE), flip_ref[0, 0] == 1)
    turned_x0 = jnp.logical_and(turned, x0)
    turned_x29 = jnp.logical_and(turned, x29)
    small = lanes(8, 128)

    def stencil(i, carry):
        rows = pl.ds(pl.multiple_of(8 * i, 8), 8)
        at = pl.multiple_of(64 * i, 64)
        wet = sub + 8 * i < depth
        half_x, half_y = 0.5 * wide(vel_ref, 0, rows), 0.5 * wide(vel_ref, 1, rows)
        to_e, to_w, to_n, to_s = D - half_x, D + half_x, D - half_y, D + half_y
        for t in range(2):
            value = jnp.where(wet, wide(tan_ref, t, rows), 0.0)
            image = mirrored(value)
            above, below = roll(value, -SIDE), roll(value, SIDE)
            east = roll(jnp.where(x0, below, value), -1)
            west = roll(jnp.where(ends, above, value), 1)
            east = jnp.where(turned_x29, image, east)
            west = jnp.where(turned_x0, image, west)
            mixed = CENTRE * value + to_e * east + to_w * west
            mixed = mixed + to_n * jnp.where(y29, 0.0, above)
            mixed = mixed + to_s * jnp.where(y0, 0.0, below)
            mixed = jnp.where(wet, mixed, 0.0)
            for c, piece in enumerate(split(mixed)):
                rhs_ref[t, pl.ds(at + 8 * c, 8), :] = piece

            answer = jnp.concatenate(
                [solved[t, pl.ds(at + 8 * c, 8), :] for c in range(CHUNKS)], axis=1
            )
            answer = jnp.where(wet, answer, 0.0)
            push_e, push_w = to_e * answer, to_w * answer
            image = mirrored(jnp.where(x29, push_e, push_w))
            moved_e, moved_w = roll(push_e, 1), roll(push_w, -1)
            straight_e = jnp.where(turned_x0, image, jnp.where(x0, 0.0, moved_e))
            straight_w = jnp.where(turned_x29, image, jnp.where(x29, 0.0, moved_w))
            cross_e = jnp.where(x0, jnp.where(turned, 0.0, moved_e), 0.0)
            cross_w = jnp.where(ends, jnp.where(turned, 0.0, moved_w), 0.0)
            inner = CENTRE * answer + straight_e + straight_w
            inner = inner + roll(to_n * answer + cross_w, SIDE)
            inner = inner + roll(to_s * answer + cross_e, -SIDE)
            inner = jnp.where(wet, inner, 0.0)
            for c, piece in enumerate(split(inner)):
                put_piece(back_ref, t, rows, c, piece)
        wet, to_n, to_s = split(wet), split(to_n), split(to_s)
        rim = (
            jnp.where(jnp.logical_and(wet[0], small < SIDE), to_s[0], 0.0),
            jnp.where(jnp.logical_and(wet[6], small >= 102), to_n[6], 0.0),
            jnp.where(jnp.logical_and(wet[7], small < 4), to_n[7], 0.0),
        )
        for number, piece in enumerate(rim):
            rim_ref[pl.ds(pl.multiple_of(64 * number + 8 * i, 8), 8), :] = piece
        return carry

    lax.fori_loop(0, GROUPS, stencil, 0)


def route_kernel(e0, e1, e2, e3, out_hbm, slots, done):
    mine = lax.shift_right_logical(lax.axis_index("tile"), 3)
    sources = (e0, e1, e2, e3)
    goals = [ref[128:129, :].astype(jnp.int32) for ref in sources]
    copies = []
    for b in range(8):
        total = jnp.zeros((128, 128), F32)
        for goal, ref in zip(goals, sources):
            total = jnp.where(goal == 8 * mine + b, ref[0:128, :], total)
        slots[b] = total
        copies.append(pltpu.make_async_copy(slots.at[b], out_hbm.at[b], done.at[b]))
        copies[-1].start()
    for copy in copies:
        copy.wait()


def finish_kernel(
    edge_ref, rhs_ref, back_hbm, rim_ref, peak_ref, link_ref,
    r0, r1, r2, r3, depth_ref, next_hbm, prev_hbm,
    right, part, solved, next_ref, prev_ref, done,
):
    fetch = pltpu.make_async_copy(back_hbm, prev_ref, done.at[2])
    fetch.start()
    depth = wide(depth_ref, slice(0, 1))
    carrier, scaled, loss = [
        sum(ref[8 * f : 8 * f + 8, :] for ref in (r0, r1, r2, r3)) for f in range(3)
    ]
    moist = scaled * jnp.exp(0.5 * peak_ref[16:24, :])
    wet = peak_ref[48:56, :] > 0.0
    heat_self = jnp.where(wet, -(0.5 * carrier + 0.25 * moist), 0.0)
    salt_heat = jnp.where(wet, 0.25 * peak_ref[24:32, :] * moist, 0.0)
    salt_self = jnp.where(wet, 0.5 * moist - loss, 0.0)
    tan_t, tan_s = peak_ref[32:40, :], peak_ref[40:48, :]
    adj_t, adj_s = peak_ref[0:8, :], peak_ref[8:16, :]

    small = lanes(8, 128)
    sub = lax.broadcasted_iota(jnp.int32, (8, WIDE), 0)

    def rims(i, carry):
        rows = pl.ds(pl.multiple_of(8 * i, 8), 8)
        at = pl.multiple_of(64 * i, 64)
        wet = split(sub + 8 * i < depth)
        rim = [rim_ref[pl.ds(pl.multiple_of(64 * n + 8 * i, 8), 8), :] for n in range(3)]
        for t in range(2):
            where = pl.ds(pl.multiple_of(64 * t + 8 * i, 8), 8)
            edge = edge_ref[0, where, :]
            for b in range(1, 8):
                edge = edge + edge_ref[b, where, :]
            north = roll(edge, 72)
            from_s, from_n = roll(edge, 68), roll(edge, 12)
            for c in range(CHUNKS):
                put = pl.ds(at + 8 * c, 8)
                value = rhs_ref[t, put, :]
                if c == 0:
                    value = value + rim[0] * edge
                elif c >= 6:
                    value = value + rim[c - 5] * north
                right[t, put, :] = value
            insides = (
                (0, jnp.logical_and(wet[0], small < SIDE), from_s),
                (6, jnp.logical_and(wet[6], small >= 102), from_n),
                (7, jnp.logical_and(wet[7], small < 4), from_n),
            )
            for c, inside, piece in insides:
                spot = slice(128 * c, min(128 * c + 128, CELLS))
                piece = jnp.where(inside, piece, 0.0)[:, 0 : spot.stop - spot.start]
                prev_ref[t, rows, spot] = prev_ref[t, rows, spot] + piece
        return carry

    fetch.wait()
    lax.fori_loop(0, GROUPS, rims, 0)
    zero = jnp.zeros((8, 128), F32)
    first = pl.ds(0, 8, stride=8)
    right[0, first, :] = right[0, first, :] + heat_self * tan_t
    right[1, first, :] = right[1, first, :] + salt_heat * tan_t + salt_self * tan_s
    adds = (heat_self * adj_t + salt_heat * adj_s, salt_self * adj_s)
    for t, add in enumerate(adds):
        for c in range(CHUNKS):
            spot = slice(128 * c, min(128 * c + 128, CELLS))
            more = add[c : c + 1, 0 : spot.stop - spot.start]
            prev_ref[t, 0:1, spot] = prev_ref[t, 0:1, spot] + more
    copy_prev = pltpu.make_async_copy(prev_ref, prev_hbm, done.at[0])
    copy_prev.start()

    def forward(i, carry):
        y_t, y_s, m = carry
        for s in range(8):
            strided = pl.ds(64 * i + s, 8, stride=8)
            packed = pl.ds(pl.multiple_of(64 * i + 8 * s, 8), 8)
            y_t = right[0, strided, :] + m * y_t
            y_s = right[1, strided, :] + m * y_s
            m = link_ref[packed, :]
            inv = link_ref[pl.ds(pl.multiple_of(512 + 64 * i + 8 * s, 8), 8), :]
            part[0, packed, :] = y_t * inv
            part[1, packed, :] = y_s * inv
        return y_t, y_s, m

    lax.fori_loop(0, GROUPS, forward, (zero, zero, zero))

    x_t = x_s = zero
    copies = [copy_prev]
    for i in reversed(range(GROUPS)):
        for s in reversed(range(8)):
            strided = pl.ds(64 * i + s, 8, stride=8)
            packed = pl.ds(64 * i + 8 * s, 8)
            m = link_ref[packed, :]
            x_t = part[0, packed, :] + m * x_t
            x_s = part[1, packed, :] + m * x_s
            solved[0, strided, :] = x_t
            solved[1, strided, :] = x_s
        rows = pl.ds(8 * i, 8)
        for t in range(2):
            for c in range(CHUNKS):
                put_piece(next_ref, t, rows, c, solved[t, pl.ds(64 * i + 8 * c, 8), :])
        copies.append(
            pltpu.make_async_copy(
                next_ref.at[:, rows, :], next_hbm.at[:, rows, :], done.at[3 + i]
            )
        )
        copies[-1].start()
    for copy in copies:
        copy.wait()


def call(kernel, name, micros, ins, outs, scratch=(), limit=VMEM_LIMIT):
    places = {"S": pltpu.SMEM, "V": pltpu.VMEM, "H": pltpu.HBM}
    shapes = [
        out if isinstance(out, jax.ShapeDtypeStruct) else jax.ShapeDtypeStruct(out, F32)
        for _, out in outs
    ]
    return pl.pallas_call(
        kernel,
        in_specs=[pl.BlockSpec(memory_space=places[place]) for place in ins],
        out_specs=[pl.BlockSpec(memory_space=places[place]) for place, _ in outs],
        out_shape=shapes,
        scratch_shapes=list(scratch),
        compiler_params=pltpu.CompilerParams(vmem_limit_bytes=limit),
        cost_estimate=pl.CostEstimate(
            flops=0, bytes_accessed=int(3.69e6 * micros), transcendentals=0
        ),
        name=name,
    )


def swap(value, axis, size, bit):
    return lax.ppermute(value, axis, [(i, i ^ bit) for i in range(size)])


def hops():
    ways = ([], [], [])
    for h in range(4):
        for low in range(2):
            step = 2 * low - 1
            targets = (((h + step) % 4, 1 - low), ((h - step) % 4, low), ((h + 2) % 4, 1 - low))
            for way, (there, low_there) in zip(ways, targets):
                for core in range(2):
                    for column in range(16):
                        source = (2 * h + core) * 32 + 2 * column + low
                        target = (2 * there + core) * 32 + 2 * column + low_there
                        way.append((source, target))
    return ways


def shards(
    tangent, adjoint, base, velocity, kappa, depth_levels, forcing, forcing_point, partner_edge,
    edge_flip,
):
    tangent, adjoint, velocity = tangent[0, 0], adjoint[0, 0], velocity[0, 0]
    base, kappa, depth = base[0, 0], kappa.reshape(Z - 1, 1, CELLS), depth_levels[0]
    mine, partner, flip = forcing_point[0], partner_edge[0], edge_flip[0]
    blocked = (2, 8 * Z, 128)
    flat = (8 * Z, 128)
    natural = (2, Z, CELLS)
    answer = (24, 128)
    line = jax.ShapeDtypeStruct((1, CELLS), jnp.int32)
    both = ("region", "tile")

    asked = [lax.ppermute(mine, both, way) for way in hops()]
    banded = forcing.reshape(8, 128, 128).transpose(1, 0, 2).reshape(1024, 128)
    edges, depth, table, solved, peak, link = call(
        solve_kernel,
        "solve",
        4.0,
        "SSHHHHHHH",
        [("V", (136, 128)), ("V", line), ("V", (384, 128))]
        + [("H", blocked), ("V", (56, 128)), ("H", (16 * Z, 128))],
        [
            pltpu.VMEM(flat, F32),
            pltpu.VMEM(blocked, F32),
            pltpu.VMEM(blocked, F32),
            pltpu.VMEM(blocked, F32),
            pltpu.VMEM((16 * Z, 128), F32),
            pltpu.VMEM(natural, F32),
            pltpu.VMEM((Z - 1, 1, CELLS), F32),
            pltpu.VMEM((1024, 128), F32),
            pltpu.VMEM(natural, F32),
            pltpu.VMEM(natural, F32),
            pltpu.VMEM((2, CELLS), F32),
            pltpu.SemaphoreType.DMA((9,)),
        ],
        limit=SOLVE_LIMIT,
    )(partner, flip, adjoint, kappa, depth, velocity, tangent, banded, base)
    table, edges, asked = lax.optimization_barrier((table, edges, asked))
    mate = swap(table, "region", 8, 1)
    edge = [edges] + [swap(edges, "tile", 32, k) for k in (8, 16, 24)]

    table, edges = lax.optimization_barrier((table, edges))
    answers = call(
        lookup_kernel,
        "lookup",
        2.7,
        "V" * 6,
        [("V", answer)] * 4,
        [pltpu.VMEM((768, 256), jnp.bfloat16)],
    )(table, mate, mine, *asked)
    replies = [answers[0]] + [
        lax.ppermute(value, both, [(target, source) for source, target in way])
        for value, way in zip(answers[1:], hops())
    ]

    edge[0], first = lax.optimization_barrier((edge[0], answers[0]))
    (slots,) = call(
        route_kernel,
        "route",
        0.9,
        "VVVV",
        [("H", (8, 128, 128))],
        [pltpu.VMEM((8, 128, 128), F32), pltpu.SemaphoreType.DMA((8,))],
    )(*edge)
    groups = [[8 * a + b for b in range(8)] for a in range(4)]
    arrived = lax.all_to_all(slots, "tile", 0, 0, axis_index_groups=groups, tiled=True)

    rhs, back, rim = call(
        stencil_kernel,
        "stencil",
        3.0,
        "SVVVV",
        [("V", blocked), ("V", natural), ("V", (192, 128))],
    )(flip, tangent, velocity, depth, solved)

    following, previous = call(
        finish_kernel,
        "finish",
        2.1,
        "VVHVVVVVVVV",
        [("H", natural), ("H", natural)],
        [
            pltpu.VMEM(blocked, F32),
            pltpu.VMEM(blocked, F32),
            pltpu.VMEM(blocked, F32),
            pltpu.VMEM(natural, F32),
            pltpu.VMEM(natural, F32),
            pltpu.SemaphoreType.DMA((11,)),
        ],
    )(arrived, rhs, back, rim, peak, link, *replies, depth)
    return following[None, None], previous[None, None]


def solution(mesh):
    fields = P("region", "tile", None, None, None)
    rows = P("region", "tile", None, None)
    single = P("region", "tile", None)
    in_specs = (fields, fields, rows, fields, rows, single, P(None, "region"), single, single, single)
    return jax.shard_map(
        shards, mesh=mesh, in_specs=in_specs, out_specs=(fields, fields), check_vma=False
    )
```

```python
import jax
import jax.numpy as jnp
from jax import lax
from jax.experimental import pallas as pl
from jax.experimental.pallas import tpu as pltpu
from jax.sharding import PartitionSpec as P

SIDE = 30
Z = 64
CELLS = SIDE * SIDE
WIDE = 1024
CHUNKS = WIDE // 128
GROUPS = Z // 8
D = 0.2
CENTRE = 1.0 - 4.0 * D
F32 = jnp.float32
SOLVE_LIMIT = 53 * 1024 * 1024 + 512 * 1024
STENCIL_LIMIT = 51 * 1024 * 1024 + 640 * 1024
VMEM_LIMIT = 8 * 1024 * 1024


def lanes(rows, width=WIDE):
    return lax.broadcasted_iota(jnp.int32, (rows, width), 1)


def split(row):
    return [row[:, 128 * c : 128 * c + 128] for c in range(CHUNKS)]


def roll(value, shift):
    return pltpu.roll(value, shift % value.shape[-1], value.ndim - 1)


def grid_masks(rows=1):
    cell = lanes(rows)
    y = lax.shift_right_logical(cell * 2185, 16)
    x = cell - y * SIDE
    return x == 0, x == SIDE - 1, y == 0, y == SIDE - 1


def mirrored(value):
    lane = lanes(value.shape[0], 128)
    back = jnp.bitwise_and(131 - lane, 127)
    turned = [jnp.take_along_axis(part, back, axis=1) for part in split(value)]
    return jnp.concatenate(
        [
            jnp.where(lane < 4, turned[7 - c], turned[max(6 - c, 0)])
            for c in range(CHUNKS)
        ],
        axis=1,
    )


def pieces_of(ref, *at):
    tail = ref[(*at, slice(WIDE - 128, CELLS))]
    fill = jnp.zeros(tail.shape[:-1] + (WIDE - CELLS,), tail.dtype)
    full = [ref[(*at, slice(128 * c, 128 * c + 128))] for c in range(CHUNKS - 1)]
    return full + [jnp.concatenate([tail, fill], axis=-1)]


def put_piece(ref, t, rows, c, value):
    if c < CHUNKS - 1:
        ref[t, rows, 128 * c : 128 * c + 128] = value
    else:
        ref[t, rows, 128 * c : CELLS] = value[:, 0 : CELLS - 128 * c]


def wide(ref, *at):
    return jnp.concatenate(pieces_of(ref, *at), axis=-1)


def make_table(forcing_ref, table_ref):
    wu, wv, ta, qa, pr, ro, ps, ic = [
        forcing_ref[pl.ds(field, 128, stride=8), :] for field in range(8)
    ]
    speed = jnp.sqrt(wu * wu + wv * wv + 1.0)
    carrier = jnp.exp(0.3 * (ps - ta)) * speed / (1.0 + jnp.exp(ic))
    table_ref[0:128, :] = carrier
    table_ref[128:256, :] = carrier * jnp.exp(-0.2 * ps)
    table_ref[256:384, :] = 0.5 * carrier * qa + pr + ro


def lookup_kernel(own_ref, mate_ref, q0, q1, q2, q3, a0, a1, a2, a3, pieces):
    band = lax.axis_index("region")
    for number, ref in enumerate((own_ref, mate_ref)):
        value = ref[...]
        coarse = value.astype(jnp.bfloat16)
        pieces[384 * number : 384 * number + 384, 0:128] = coarse
        pieces[384 * number : 384 * number + 384, 128:256] = (
            value - coarse.astype(F32)
        ).astype(jnp.bfloat16)
    base_own = band * 128
    base_mate = (band + 1 - 2 * lax.rem(band, 2)) * 128
    low = jnp.bitwise_and(lax.broadcasted_iota(jnp.int32, (256, 256), 0), 127)
    high = lax.broadcasted_iota(jnp.int32, (128, 256), 0)
    for q_ref, a_ref in ((q0, a0), (q1, a1), (q2, a2), (q3, a3)):
        points = pieces_of(q_ref, slice(0, 1))
        for part in range(4):
            point = jnp.concatenate(points[2 * part : 2 * part + 2], axis=1)
            onehot = (low == jnp.bitwise_and(point, 127)).astype(jnp.bfloat16)
            found = jnp.dot(pieces[...], onehot, preferred_element_type=F32)
            row = lax.shift_right_logical(point, 7)
            here = high == row - base_own
            there = high == row - base_mate
            for field in range(3):
                picked = jnp.where(here, found[128 * field : 128 * field + 128], 0.0)
                picked = picked + jnp.where(
                    there, found[384 + 128 * field : 512 + 128 * field], 0.0
                )
                total = jnp.sum(picked, axis=0, keepdims=True)
                at = 8 * field + 2 * part
                a_ref[at : at + 1, :] = total[:, 0:128]
                a_ref[at + 1 : at + 2, :] = total[:, 128:256]


def solve_kernel(
    partner_ref, flip_ref, adj_hbm, kap_hbm, depth_hbm, vel_hbm, tan_hbm, forcing_hbm, base_hbm,
    edge_ref, depth_ref, table_ref, solved_hbm, peak_ref, link_hbm,
    coup, given, part, solved, link_ref, adj_ref, kap_ref, forcing_ref, vel_ref, tan_ref, base_ref, done,
):
    copies = [
        pltpu.make_async_copy(source, target, done.at[number])
        for number, (source, target) in enumerate(
            (
                (kap_hbm, kap_ref),
                (depth_hbm, depth_ref),
                (adj_hbm, adj_ref),
                (forcing_hbm, forcing_ref),
                (vel_hbm, vel_ref),
                (tan_hbm, tan_ref),
                (base_hbm, base_ref),
            )
        )
    ]
    for copy in copies:
        copy.start()
    copies[0].wait()
    copies[1].wait()
    depths = pieces_of(depth_ref, slice(0, 1))
    for level in range(Z - 1):
        for c, piece in enumerate(pieces_of(kap_ref, level, slice(0, 1))):
            coup[8 * level + c : 8 * level + c + 1, :] = piece
    coup[8 * Z - 8 :, :] = jnp.zeros((8, 128), F32)
    for c, piece in enumerate(depths):
        peak_ref[c : c + 1, :] = piece.astype(F32)
    columns = peak_ref[0:8, :].astype(jnp.int32)

    copies[2].wait()

    def relayout(i, carry):
        rows = pl.ds(pl.multiple_of(8 * i, 8), 8)
        at = pl.multiple_of(64 * i, 64)
        for t in range(2):
            for c, piece in enumerate(pieces_of(adj_ref, t, rows)):
                given[t, pl.ds(at + 8 * c, 8), :] = piece
        return carry

    lax.fori_loop(0, GROUPS, relayout, 0)

    def forward(i, carry):
        e, y_t, y_s, m = carry
        for s in range(8):
            strided = pl.ds(64 * i + s, 8, stride=8)
            packed = pl.ds(pl.multiple_of(64 * i + 8 * s, 8), 8)
            link = jnp.where(8 * i + s + 1 < columns, coup[packed, :], 0.0)
            inv = 1.0 / (e + link)
            y_t = given[0, strided, :] + m * y_t
            y_s = given[1, strided, :] + m * y_s
            m = link * inv
            e = 1.0 + m * e
            link_ref[pl.ds(pl.multiple_of(512 + 64 * i + 8 * s, 8), 8), :] = inv
            link_ref[packed, :] = m
            part[0, packed, :] = y_t * inv
            part[1, packed, :] = y_s * inv
        return e, y_t, y_s, m

    zero = jnp.zeros((8, 128), F32)
    lax.fori_loop(0, GROUPS, forward, (zero + 1.0, zero, zero, zero))
    keep_link = pltpu.make_async_copy(link_ref, link_hbm, done.at[8])
    keep_link.start()

    def backward(n, carry):
        x_t, x_s = carry
        i = GROUPS - 1 - n
        for s in reversed(range(8)):
            strided = pl.ds(64 * i + s, 8, stride=8)
            packed = pl.ds(pl.multiple_of(64 * i + 8 * s, 8), 8)
            m = link_ref[packed, :]
            x_t = part[0, packed, :] + m * x_t
            x_s = part[1, packed, :] + m * x_s
            solved[0, strided, :] = x_t
            solved[1, strided, :] = x_s
        return x_t, x_s

    x_t, x_s = lax.fori_loop(0, GROUPS, backward, (zero, zero))
    peak_ref[0:8, :] = x_t
    peak_ref[8:16, :] = x_s
    keep = pltpu.make_async_copy(solved, solved_hbm, done.at[7])
    keep.start()
    copies[3].wait()
    make_table(forcing_ref, table_ref)
    for copy in copies[4:]:
        copy.wait()
    for t in range(2):
        for c, piece in enumerate(pieces_of(base_ref, slice(t, t + 1))):
            peak_ref[16 + 8 * t + c : 17 + 8 * t + c, :] = piece
        for c, piece in enumerate(pieces_of(tan_ref, t, slice(0, 1))):
            wet = depths[c] > 0
            peak_ref[32 + 8 * t + c : 33 + 8 * t + c, :] = jnp.where(wet, piece, 0.0)
    for c, piece in enumerate(depths):
        peak_ref[48 + c : 49 + c, :] = piece.astype(F32)

    small = lanes(8, 128)
    south, north = flip_ref[0, 2] == 1, flip_ref[0, 3] == 1
    order = small
    for first, turn in ((0, south), (30, north), (60, south), (90, north)):
        inside = jnp.logical_and(small >= first, small < first + SIDE)
        order = jnp.where(
            jnp.logical_and(inside, turn), 2 * first + SIDE - 1 - small, order
        )
    upper = small >= 102
    level = lax.broadcasted_iota(jnp.int32, (8, 128), 0)

    def pack(i, carry):
        rows = pl.ds(pl.multiple_of(8 * i, 8), 8)
        at = pl.multiple_of(64 * i, 64)
        wet = {c: level + 8 * i < depths[c] for c in (0, 6, 7)}
        speed = pieces_of(vel_ref, 1, rows)
        half = {c: 0.5 * speed[c] for c in (0, 6, 7)}
        for t in range(2):
            value, push = {}, {}
            tracer = pieces_of(tan_ref, t, rows)
            for c in (0, 6, 7):
                value[c] = jnp.where(wet[c], tracer[c], 0.0)
                factor = D + half[c] if c == 0 else D - half[c]
                push[c] = jnp.where(
                    wet[c], factor * solved[t, pl.ds(at + 8 * c, 8), :], 0.0
                )
            edges = jnp.where(small < 30, value[0], 0.0)
            packs = (
                (roll(jnp.where(upper, value[6], value[7]), 56), 30),
                (roll(push[0], 60), 60),
                (roll(jnp.where(upper, push[6], push[7]), 116), 90),
            )
            for piece, first in packs:
                inside = jnp.logical_and(small >= first, small < first + SIDE)
                edges = jnp.where(inside, piece, edges)
            edges = jnp.take_along_axis(edges, order, axis=1)
            edge_ref[pl.ds(pl.multiple_of(64 * t + 8 * i, 8), 8), :] = edges
        return carry

    lax.fori_loop(0, GROUPS, pack, 0, unroll=4)
    second = jnp.logical_or(small < 30, jnp.logical_and(small >= 60, small < 90))
    target = jnp.where(
        second,
        lax.shift_right_logical(partner_ref[0, 2], 2),
        lax.shift_right_logical(partner_ref[0, 3], 2),
    )
    edge_ref[128:136, :] = jnp.where(small < 120, target, -1).astype(F32)
    keep.wait()
    keep_link.wait()


def stencil_kernel(
    flip_ref, tan_ref, vel_ref, depth_ref, solved_hbm, rhs_ref, back_ref, rim_ref,
    solved, done,
):
    fetch = pltpu.make_async_copy(solved_hbm, solved, done.at[0])
    fetch.start()
    depth = wide(depth_ref, slice(0, 1))
    sub = lax.broadcasted_iota(jnp.int32, (8, WIDE), 0)
    x0, x29, y0, y29 = grid_masks(8)
    ends = jnp.logical_or(x29, lanes(8) == WIDE - 1)
    turned = jnp.full((8, WIDE), flip_ref[0, 0] == 1)
    turned_x0 = jnp.logical_and(turned, x0)
    turned_x29 = jnp.logical_and(turned, x29)
    small = lanes(8, 128)

    def stencil(i, carry):
        rows = pl.ds(pl.multiple_of(8 * i, 8), 8)
        at = pl.multiple_of(64 * i, 64)
        wet = sub + 8 * i < depth
        half_x, half_y = 0.5 * wide(vel_ref, 0, rows), 0.5 * wide(vel_ref, 1, rows)
        to_e, to_w, to_n, to_s = D - half_x, D + half_x, D - half_y, D + half_y
        for t in range(2):
            value = jnp.where(wet, wide(tan_ref, t, rows), 0.0)
            image = mirrored(value)
            above, below = roll(value, -SIDE), roll(value, SIDE)
            east = roll(jnp.where(x0, below, value), -1)
            west = roll(jnp.where(ends, above, value), 1)
            east = jnp.where(turned_x29, image, east)
            west = jnp.where(turned_x0, image, west)
            mixed = CENTRE * value + to_e * east + to_w * west
            mixed = mixed + to_n * jnp.where(y29, 0.0, above)
            mixed = mixed + to_s * jnp.where(y0, 0.0, below)
            mixed = jnp.where(wet, mixed, 0.0)
            for c, piece in enumerate(split(mixed)):
                rhs_ref[t, pl.ds(at + 8 * c, 8), :] = piece
        wet, to_n, to_s = split(wet), split(to_n), split(to_s)
        rim = (
            jnp.where(jnp.logical_and(wet[0], small < SIDE), to_s[0], 0.0),
            jnp.where(jnp.logical_and(wet[6], small >= 102), to_n[6], 0.0),
            jnp.where(jnp.logical_and(wet[7], small < 4), to_n[7], 0.0),
        )
        for number, piece in enumerate(rim):
            rim_ref[pl.ds(pl.multiple_of(64 * number + 8 * i, 8), 8), :] = piece
        return carry

    lax.fori_loop(0, GROUPS, stencil, 0)
    fetch.wait()

    def adjoint(i, carry):
        rows = pl.ds(pl.multiple_of(8 * i, 8), 8)
        at = pl.multiple_of(64 * i, 64)
        wet = sub + 8 * i < depth
        half_x, half_y = 0.5 * wide(vel_ref, 0, rows), 0.5 * wide(vel_ref, 1, rows)
        to_e, to_w, to_n, to_s = D - half_x, D + half_x, D - half_y, D + half_y
        for t in range(2):
            answer = jnp.concatenate(
                [solved[t, pl.ds(at + 8 * c, 8), :] for c in range(CHUNKS)], axis=1
            )
            answer = jnp.where(wet, answer, 0.0)
            push_e, push_w = to_e * answer, to_w * answer
            image = mirrored(jnp.where(x29, push_e, push_w))
            moved_e, moved_w = roll(push_e, 1), roll(push_w, -1)
            straight_e = jnp.where(turned_x0, image, jnp.where(x0, 0.0, moved_e))
            straight_w = jnp.where(turned_x29, image, jnp.where(x29, 0.0, moved_w))
            cross_e = jnp.where(x0, jnp.where(turned, 0.0, moved_e), 0.0)
            cross_w = jnp.where(ends, jnp.where(turned, 0.0, moved_w), 0.0)
            inner = CENTRE * answer + straight_e + straight_w
            inner = inner + roll(to_n * answer + cross_w, SIDE)
            inner = inner + roll(to_s * answer + cross_e, -SIDE)
            inner = jnp.where(wet, inner, 0.0)
            for c, piece in enumerate(split(inner)):
                put_piece(back_ref, t, rows, c, piece)
        return carry

    lax.fori_loop(0, GROUPS, adjoint, 0)


def route_kernel(e0, e1, e2, e3, out_hbm, slots, done):
    mine = lax.shift_right_logical(lax.axis_index("tile"), 3)
    sources = (e0, e1, e2, e3)
    goals = [ref[128:129, :].astype(jnp.int32) for ref in sources]
    copies = []
    for b in range(8):
        total = jnp.zeros((128, 128), F32)
        for goal, ref in zip(goals, sources):
            total = jnp.where(goal == 8 * mine + b, ref[0:128, :], total)
        slots[b] = total
        copies.append(pltpu.make_async_copy(slots.at[b], out_hbm.at[b], done.at[b]))
        copies[-1].start()
    for copy in copies:
        copy.wait()


def finish_kernel(
    edge_ref, rhs_ref, back_hbm, rim_ref, peak_ref, link_ref,
    r0, r1, r2, r3, depth_ref, next_hbm, prev_hbm,
    right, part, solved, next_ref, prev_ref, done,
):
    fetch = pltpu.make_async_copy(back_hbm, prev_ref, done.at[2])
    fetch.start()
    depth = wide(depth_ref, slice(0, 1))
    carrier, scaled, loss = [
        sum(ref[8 * f : 8 * f + 8, :] for ref in (r0, r1, r2, r3)) for f in range(3)
    ]
    moist = scaled * jnp.exp(0.5 * peak_ref[16:24, :])
    wet = peak_ref[48:56, :] > 0.0
    heat_self = jnp.where(wet, -(0.5 * carrier + 0.25 * moist), 0.0)
    salt_heat = jnp.where(wet, 0.25 * peak_ref[24:32, :] * moist, 0.0)
    salt_self = jnp.where(wet, 0.5 * moist - loss, 0.0)
    tan_t, tan_s = peak_ref[32:40, :], peak_ref[40:48, :]
    adj_t, adj_s = peak_ref[0:8, :], peak_ref[8:16, :]

    small = lanes(8, 128)
    sub = lax.broadcasted_iota(jnp.int32, (8, WIDE), 0)

    def rims(i, carry):
        rows = pl.ds(pl.multiple_of(8 * i, 8), 8)
        at = pl.multiple_of(64 * i, 64)
        wet = split(sub + 8 * i < depth)
        rim = [rim_ref[pl.ds(pl.multiple_of(64 * n + 8 * i, 8), 8), :] for n in range(3)]
        for t in range(2):
            where = pl.ds(pl.multiple_of(64 * t + 8 * i, 8), 8)
            edge = edge_ref[0, where, :]
            for b in range(1, 8):
                edge = edge + edge_ref[b, where, :]
            north = roll(edge, 72)
            from_s, from_n = roll(edge, 68), roll(edge, 12)
            for c in range(CHUNKS):
                put = pl.ds(at + 8 * c, 8)
                value = rhs_ref[t, put, :]
                if c == 0:
                    value = value + rim[0] * edge
                elif c >= 6:
                    value = value + rim[c - 5] * north
                right[t, put, :] = value
            insides = (
                (0, jnp.logical_and(wet[0], small < SIDE), from_s),
                (6, jnp.logical_and(wet[6], small >= 102), from_n),
                (7, jnp.logical_and(wet[7], small < 4), from_n),
            )
            for c, inside, piece in insides:
                spot = slice(128 * c, min(128 * c + 128, CELLS))
                piece = jnp.where(inside, piece, 0.0)[:, 0 : spot.stop - spot.start]
                prev_ref[t, rows, spot] = prev_ref[t, rows, spot] + piece
        return carry

    fetch.wait()
    lax.fori_loop(0, GROUPS, rims, 0)
    zero = jnp.zeros((8, 128), F32)
    first = pl.ds(0, 8, stride=8)
    right[0, first, :] = right[0, first, :] + heat_self * tan_t
    right[1, first, :] = right[1, first, :] + salt_heat * tan_t + salt_self * tan_s
    adds = (heat_self * adj_t + salt_heat * adj_s, salt_self * adj_s)
    for t, add in enumerate(adds):
        for c in range(CHUNKS):
            spot = slice(128 * c, min(128 * c + 128, CELLS))
            more = add[c : c + 1, 0 : spot.stop - spot.start]
            prev_ref[t, 0:1, spot] = prev_ref[t, 0:1, spot] + more
    copy_prev = pltpu.make_async_copy(prev_ref, prev_hbm, done.at[0])
    copy_prev.start()

    def forward(i, carry):
        y_t, y_s, m = carry
        for s in range(8):
            strided = pl.ds(64 * i + s, 8, stride=8)
            packed = pl.ds(pl.multiple_of(64 * i + 8 * s, 8), 8)
            y_t = right[0, strided, :] + m * y_t
            y_s = right[1, strided, :] + m * y_s
            m = link_ref[packed, :]
            inv = link_ref[pl.ds(pl.multiple_of(512 + 64 * i + 8 * s, 8), 8), :]
            part[0, packed, :] = y_t * inv
            part[1, packed, :] = y_s * inv
        return y_t, y_s, m

    lax.fori_loop(0, GROUPS, forward, (zero, zero, zero))

    x_t = x_s = zero
    copies = [copy_prev]
    for i in reversed(range(GROUPS)):
        for s in reversed(range(8)):
            strided = pl.ds(64 * i + s, 8, stride=8)
            packed = pl.ds(64 * i + 8 * s, 8)
            m = link_ref[packed, :]
            x_t = part[0, packed, :] + m * x_t
            x_s = part[1, packed, :] + m * x_s
            solved[0, strided, :] = x_t
            solved[1, strided, :] = x_s
        rows = pl.ds(8 * i, 8)
        for t in range(2):
            for c in range(CHUNKS):
                put_piece(next_ref, t, rows, c, solved[t, pl.ds(64 * i + 8 * c, 8), :])
        copies.append(
            pltpu.make_async_copy(
                next_ref.at[:, rows, :], next_hbm.at[:, rows, :], done.at[3 + i]
            )
        )
        copies[-1].start()
    for copy in copies:
        copy.wait()


def call(kernel, name, micros, ins, outs, scratch=(), limit=VMEM_LIMIT):
    places = {"S": pltpu.SMEM, "V": pltpu.VMEM, "H": pltpu.HBM}
    shapes = [
        out if isinstance(out, jax.ShapeDtypeStruct) else jax.ShapeDtypeStruct(out, F32)
        for _, out in outs
    ]
    return pl.pallas_call(
        kernel,
        in_specs=[pl.BlockSpec(memory_space=places[place]) for place in ins],
        out_specs=[pl.BlockSpec(memory_space=places[place]) for place, _ in outs],
        out_shape=shapes,
        scratch_shapes=list(scratch),
        compiler_params=pltpu.CompilerParams(vmem_limit_bytes=limit),
        cost_estimate=pl.CostEstimate(
            flops=0, bytes_accessed=int(3.69e6 * micros), transcendentals=0
        ),
        name=name,
    )


def swap(value, axis, size, bit):
    return lax.ppermute(value, axis, [(i, i ^ bit) for i in range(size)])


def hops():
    ways = ([], [], [])
    for h in range(4):
        for low in range(2):
            step = 2 * low - 1
            targets = (((h + step) % 4, 1 - low), ((h - step) % 4, low), ((h + 2) % 4, 1 - low))
            for way, (there, low_there) in zip(ways, targets):
                for core in range(2):
                    for column in range(16):
                        source = (2 * h + core) * 32 + 2 * column + low
                        target = (2 * there + core) * 32 + 2 * column + low_there
                        way.append((source, target))
    return ways


def shards(
    tangent, adjoint, base, velocity, kappa, depth_levels, forcing, forcing_point, partner_edge,
    edge_flip,
):
    tangent, adjoint, velocity = tangent[0, 0], adjoint[0, 0], velocity[0, 0]
    base, kappa, depth = base[0, 0], kappa.reshape(Z - 1, 1, CELLS), depth_levels[0]
    mine, partner, flip = forcing_point[0], partner_edge[0], edge_flip[0]
    blocked = (2, 8 * Z, 128)
    flat = (8 * Z, 128)
    natural = (2, Z, CELLS)
    answer = (24, 128)
    line = jax.ShapeDtypeStruct((1, CELLS), jnp.int32)
    both = ("region", "tile")

    asked = [lax.ppermute(mine, both, way) for way in hops()]
    banded = forcing.reshape(8, 128, 128).transpose(1, 0, 2).reshape(1024, 128)
    edges, depth, table, solved, peak, link = call(
        solve_kernel,
        "solve",
        4.0,
        "SSHHHHHHH",
        [("V", (136, 128)), ("V", line), ("V", (384, 128))]
        + [("H", blocked), ("V", (56, 128)), ("H", (16 * Z, 128))],
        [
            pltpu.VMEM(flat, F32),
            pltpu.VMEM(blocked, F32),
            pltpu.VMEM(blocked, F32),
            pltpu.VMEM(blocked, F32),
            pltpu.VMEM((16 * Z, 128), F32),
            pltpu.VMEM(natural, F32),
            pltpu.VMEM((Z - 1, 1, CELLS), F32),
            pltpu.VMEM((1024, 128), F32),
            pltpu.VMEM(natural, F32),
            pltpu.VMEM(natural, F32),
            pltpu.VMEM((2, CELLS), F32),
            pltpu.SemaphoreType.DMA((9,)),
        ],
        limit=SOLVE_LIMIT,
    )(partner, flip, adjoint, kappa, depth, velocity, tangent, banded, base)
    table, edges, asked = lax.optimization_barrier((table, edges, asked))
    mate = swap(table, "region", 8, 1)
    edge = [edges] + [swap(edges, "tile", 32, k) for k in (8, 16, 24)]

    table, edges = lax.optimization_barrier((table, edges))
    answers = call(
        lookup_kernel,
        "lookup",
        2.7,
        "V" * 6,
        [("V", answer)] * 4,
        [pltpu.VMEM((768, 256), jnp.bfloat16)],
    )(table, mate, mine, *asked)
    replies = [answers[0]] + [
        lax.ppermute(value, both, [(target, source) for source, target in way])
        for value, way in reversed(list(zip(answers[1:], hops())))
    ]

    edge[0], first = lax.optimization_barrier((edge[0], answers[0]))
    (slots,) = call(
        route_kernel,
        "route",
        0.9,
        "VVVV",
        [("H", (8, 128, 128))],
        [pltpu.VMEM((8, 128, 128), F32), pltpu.SemaphoreType.DMA((8,))],
    )(*edge)
    groups = [[8 * a + b for b in range(8)] for a in range(4)]
    arrived = lax.all_to_all(slots, "tile", 0, 0, axis_index_groups=groups, tiled=True)

    rhs, back, rim = call(
        stencil_kernel,
        "stencil",
        3.0,
        "SVVVH",
        [("V", blocked), ("V", natural), ("V", (192, 128))],
        [pltpu.VMEM(blocked, F32), pltpu.SemaphoreType.DMA((1,))],
        limit=STENCIL_LIMIT,
    )(flip, tangent, velocity, depth, solved)

    following, previous = call(
        finish_kernel,
        "finish",
        2.1,
        "VVHVVVVVVVV",
        [("H", natural), ("H", natural)],
        [
            pltpu.VMEM(blocked, F32),
            pltpu.VMEM(blocked, F32),
            pltpu.VMEM(blocked, F32),
            pltpu.VMEM(natural, F32),
            pltpu.VMEM(natural, F32),
            pltpu.SemaphoreType.DMA((11,)),
        ],
    )(arrived, rhs, back, rim, peak, link, *replies, depth)
    return following[None, None], previous[None, None]


def solution(mesh):
    fields = P("region", "tile", None, None, None)
    rows = P("region", "tile", None, None)
    single = P("region", "tile", None)
    in_specs = (fields, fields, rows, fields, rows, single, P(None, "region"), single, single, single)
    return jax.shard_map(
        shards, mesh=mesh, in_specs=in_specs, out_specs=(fields, fields), check_vma=False
    )
```

```python
import jax
import jax.numpy as jnp
from jax import lax
from jax.experimental import pallas as pl
from jax.experimental.pallas import tpu as pltpu
from jax.sharding import PartitionSpec as P

SIDE = 30
Z = 64
CELLS = SIDE * SIDE
WIDE = 1024
CHUNKS = WIDE // 128
GROUPS = Z // 8
D = 0.2
CENTRE = 1.0 - 4.0 * D
F32 = jnp.float32
SOLVE_LIMIT = 53 * 1024 * 1024 + 512 * 1024
STENCIL_LIMIT = 51 * 1024 * 1024 + 640 * 1024
VMEM_LIMIT = 8 * 1024 * 1024


def lanes(rows, width=WIDE):
    return lax.broadcasted_iota(jnp.int32, (rows, width), 1)


def split(row):
    return [row[:, 128 * c : 128 * c + 128] for c in range(CHUNKS)]


def roll(value, shift):
    return pltpu.roll(value, shift % value.shape[-1], value.ndim - 1)


def grid_masks(rows=1):
    cell = lanes(rows)
    y = lax.shift_right_logical(cell * 2185, 16)
    x = cell - y * SIDE
    return x == 0, x == SIDE - 1, y == 0, y == SIDE - 1


def mirrored(value):
    lane = lanes(value.shape[0], 128)
    back = jnp.bitwise_and(131 - lane, 127)
    turned = [jnp.take_along_axis(part, back, axis=1) for part in split(value)]
    return jnp.concatenate(
        [
            jnp.where(lane < 4, turned[7 - c], turned[max(6 - c, 0)])
            for c in range(CHUNKS)
        ],
        axis=1,
    )


def pieces_of(ref, *at):
    tail = ref[(*at, slice(WIDE - 128, CELLS))]
    fill = jnp.zeros(tail.shape[:-1] + (WIDE - CELLS,), tail.dtype)
    full = [ref[(*at, slice(128 * c, 128 * c + 128))] for c in range(CHUNKS - 1)]
    return full + [jnp.concatenate([tail, fill], axis=-1)]


def put_piece(ref, t, rows, c, value):
    if c < CHUNKS - 1:
        ref[t, rows, 128 * c : 128 * c + 128] = value
    else:
        ref[t, rows, 128 * c : CELLS] = value[:, 0 : CELLS - 128 * c]


def wide(ref, *at):
    return jnp.concatenate(pieces_of(ref, *at), axis=-1)


def make_table(forcing_ref, table_ref):
    wu, wv, ta, qa, pr, ro, ps, ic = [
        forcing_ref[pl.ds(field, 128, stride=8), :] for field in range(8)
    ]
    speed = jnp.sqrt(wu * wu + wv * wv + 1.0)
    carrier = jnp.exp(0.3 * (ps - ta)) * speed / (1.0 + jnp.exp(ic))
    table_ref[0:128, :] = carrier
    table_ref[128:256, :] = carrier * jnp.exp(-0.2 * ps)
    table_ref[256:384, :] = 0.5 * carrier * qa + pr + ro


def lookup_kernel(own_ref, mate_ref, q0, q1, q2, q3, a0, a1, a2, a3, pieces):
    band = lax.axis_index("region")
    for number, ref in enumerate((own_ref, mate_ref)):
        value = ref[...]
        coarse = value.astype(jnp.bfloat16)
        pieces[384 * number : 384 * number + 384, 0:128] = coarse
        pieces[384 * number : 384 * number + 384, 128:256] = (
            value - coarse.astype(F32)
        ).astype(jnp.bfloat16)
    base_own = band * 128
    base_mate = (band + 1 - 2 * lax.rem(band, 2)) * 128
    low = jnp.bitwise_and(lax.broadcasted_iota(jnp.int32, (256, 256), 0), 127)
    high = lax.broadcasted_iota(jnp.int32, (128, 256), 0)
    for q_ref, a_ref in ((q0, a0), (q1, a1), (q2, a2), (q3, a3)):
        points = pieces_of(q_ref, slice(0, 1))
        for part in range(4):
            point = jnp.concatenate(points[2 * part : 2 * part + 2], axis=1)
            onehot = (low == jnp.bitwise_and(point, 127)).astype(jnp.bfloat16)
            found = jnp.dot(pieces[...], onehot, preferred_element_type=F32)
            row = lax.shift_right_logical(point, 7)
            here = high == row - base_own
            there = high == row - base_mate
            for field in range(3):
                picked = jnp.where(here, found[128 * field : 128 * field + 128], 0.0)
                picked = picked + jnp.where(
                    there, found[384 + 128 * field : 512 + 128 * field], 0.0
                )
                total = jnp.sum(picked, axis=0, keepdims=True)
                at = 8 * field + 2 * part
                a_ref[at : at + 1, :] = total[:, 0:128]
                a_ref[at + 1 : at + 2, :] = total[:, 128:256]


def solve_kernel(
    partner_ref, flip_ref, adj_hbm, kap_hbm, depth_hbm, vel_hbm, tan_hbm, forcing_hbm, base_hbm,
    edge_ref, depth_ref, table_ref, solved_hbm, peak_ref, link_hbm,
    coup, given, part, solved, link_ref, adj_ref, kap_ref, forcing_ref, vel_ref, tan_ref, base_ref, done,
):
    copies = [
        pltpu.make_async_copy(source, target, done.at[number])
        for number, (source, target) in enumerate(
            (
                (kap_hbm, kap_ref),
                (depth_hbm, depth_ref),
                (adj_hbm, adj_ref),
                (forcing_hbm, forcing_ref),
                (vel_hbm, vel_ref),
                (tan_hbm, tan_ref),
                (base_hbm, base_ref),
            )
        )
    ]
    for copy in copies:
        copy.start()
    copies[0].wait()
    copies[1].wait()
    depths = pieces_of(depth_ref, slice(0, 1))
    for level in range(Z - 1):
        for c, piece in enumerate(pieces_of(kap_ref, level, slice(0, 1))):
            coup[8 * level + c : 8 * level + c + 1, :] = piece
    coup[8 * Z - 8 :, :] = jnp.zeros((8, 128), F32)
    for c, piece in enumerate(depths):
        peak_ref[c : c + 1, :] = piece.astype(F32)
    columns = peak_ref[0:8, :].astype(jnp.int32)

    copies[2].wait()

    def relayout(i, carry):
        rows = pl.ds(pl.multiple_of(8 * i, 8), 8)
        at = pl.multiple_of(64 * i, 64)
        for t in range(2):
            for c, piece in enumerate(pieces_of(adj_ref, t, rows)):
                given[t, pl.ds(at + 8 * c, 8), :] = piece
        return carry

    lax.fori_loop(0, GROUPS, relayout, 0)

    def forward(i, carry):
        e, y_t, y_s, m = carry
        for s in range(8):
            strided = pl.ds(64 * i + s, 8, stride=8)
            packed = pl.ds(pl.multiple_of(64 * i + 8 * s, 8), 8)
            link = jnp.where(8 * i + s + 1 < columns, coup[packed, :], 0.0)
            inv = 1.0 / (e + link)
            y_t = given[0, strided, :] + m * y_t
            y_s = given[1, strided, :] + m * y_s
            m = link * inv
            e = 1.0 + m * e
            link_ref[pl.ds(pl.multiple_of(512 + 64 * i + 8 * s, 8), 8), :] = inv
            link_ref[packed, :] = m
            part[0, packed, :] = y_t * inv
            part[1, packed, :] = y_s * inv
        return e, y_t, y_s, m

    zero = jnp.zeros((8, 128), F32)
    lax.fori_loop(0, GROUPS, forward, (zero + 1.0, zero, zero, zero))
    keep_link = pltpu.make_async_copy(link_ref, link_hbm, done.at[8])
    keep_link.start()

    def backward(n, carry):
        x_t, x_s = carry
        i = GROUPS - 1 - n
        for s in reversed(range(8)):
            strided = pl.ds(64 * i + s, 8, stride=8)
            packed = pl.ds(pl.multiple_of(64 * i + 8 * s, 8), 8)
            m = link_ref[packed, :]
            x_t = part[0, packed, :] + m * x_t
            x_s = part[1, packed, :] + m * x_s
            solved[0, strided, :] = x_t
            solved[1, strided, :] = x_s
        return x_t, x_s

    x_t, x_s = lax.fori_loop(0, GROUPS, backward, (zero, zero))
    peak_ref[0:8, :] = x_t
    peak_ref[8:16, :] = x_s
    keep = pltpu.make_async_copy(solved, solved_hbm, done.at[7])
    keep.start()
    copies[3].wait()
    make_table(forcing_ref, table_ref)
    for copy in copies[4:]:
        copy.wait()
    for t in range(2):
        for c, piece in enumerate(pieces_of(base_ref, slice(t, t + 1))):
            peak_ref[16 + 8 * t + c : 17 + 8 * t + c, :] = piece
        for c, piece in enumerate(pieces_of(tan_ref, t, slice(0, 1))):
            wet = depths[c] > 0
            peak_ref[32 + 8 * t + c : 33 + 8 * t + c, :] = jnp.where(wet, piece, 0.0)
    for c, piece in enumerate(depths):
        peak_ref[48 + c : 49 + c, :] = piece.astype(F32)

    small = lanes(8, 128)
    south, north = flip_ref[0, 2] == 1, flip_ref[0, 3] == 1
    order = small
    for first, turn in ((0, south), (30, north), (60, south), (90, north)):
        inside = jnp.logical_and(small >= first, small < first + SIDE)
        order = jnp.where(
            jnp.logical_and(inside, turn), 2 * first + SIDE - 1 - small, order
        )
    upper = small >= 102
    level = lax.broadcasted_iota(jnp.int32, (8, 128), 0)

    def pack(i, carry):
        rows = pl.ds(pl.multiple_of(8 * i, 8), 8)
        at = pl.multiple_of(64 * i, 64)
        wet = {c: level + 8 * i < depths[c] for c in (0, 6, 7)}
        speed = pieces_of(vel_ref, 1, rows)
        half = {c: 0.5 * speed[c] for c in (0, 6, 7)}
        for t in range(2):
            value, push = {}, {}
            tracer = pieces_of(tan_ref, t, rows)
            for c in (0, 6, 7):
                value[c] = jnp.where(wet[c], tracer[c], 0.0)
                factor = D + half[c] if c == 0 else D - half[c]
                push[c] = jnp.where(
                    wet[c], factor * solved[t, pl.ds(at + 8 * c, 8), :], 0.0
                )
            edges = jnp.where(small < 30, value[0], 0.0)
            packs = (
                (roll(jnp.where(upper, value[6], value[7]), 56), 30),
                (roll(push[0], 60), 60),
                (roll(jnp.where(upper, push[6], push[7]), 116), 90),
            )
            for piece, first in packs:
                inside = jnp.logical_and(small >= first, small < first + SIDE)
                edges = jnp.where(inside, piece, edges)
            edges = jnp.take_along_axis(edges, order, axis=1)
            edge_ref[pl.ds(pl.multiple_of(64 * t + 8 * i, 8), 8), :] = edges
        return carry

    lax.fori_loop(0, GROUPS, pack, 0, unroll=True)
    second = jnp.logical_or(small < 30, jnp.logical_and(small >= 60, small < 90))
    target = jnp.where(
        second,
        lax.shift_right_logical(partner_ref[0, 2], 2),
        lax.shift_right_logical(partner_ref[0, 3], 2),
    )
    edge_ref[128:136, :] = jnp.where(small < 120, target, -1).astype(F32)
    keep.wait()
    keep_link.wait()


def stencil_kernel(
    flip_ref, tan_ref, vel_ref, depth_ref, solved_hbm, rhs_ref, back_ref, rim_ref,
    solved, done,
):
    fetch = pltpu.make_async_copy(solved_hbm, solved, done.at[0])
    fetch.start()
    depth = wide(depth_ref, slice(0, 1))
    sub = lax.broadcasted_iota(jnp.int32, (8, WIDE), 0)
    x0, x29, y0, y29 = grid_masks(8)
    ends = jnp.logical_or(x29, lanes(8) == WIDE - 1)
    turned = jnp.full((8, WIDE), flip_ref[0, 0] == 1)
    turned_x0 = jnp.logical_and(turned, x0)
    turned_x29 = jnp.logical_and(turned, x29)
    small = lanes(8, 128)

    def stencil(i, carry):
        rows = pl.ds(pl.multiple_of(8 * i, 8), 8)
        at = pl.multiple_of(64 * i, 64)
        wet = sub + 8 * i < depth
        half_x, half_y = 0.5 * wide(vel_ref, 0, rows), 0.5 * wide(vel_ref, 1, rows)
        to_e, to_w, to_n, to_s = D - half_x, D + half_x, D - half_y, D + half_y
        for t in range(2):
            value = jnp.where(wet, wide(tan_ref, t, rows), 0.0)
            image = mirrored(value)
            above, below = roll(value, -SIDE), roll(value, SIDE)
            east = roll(jnp.where(x0, below, value), -1)
            west = roll(jnp.where(ends, above, value), 1)
            east = jnp.where(turned_x29, image, east)
            west = jnp.where(turned_x0, image, west)
            mixed = CENTRE * value + to_e * east + to_w * west
            mixed = mixed + to_n * jnp.where(y29, 0.0, above)
            mixed = mixed + to_s * jnp.where(y0, 0.0, below)
            mixed = jnp.where(wet, mixed, 0.0)
            for c, piece in enumerate(split(mixed)):
                rhs_ref[t, pl.ds(at + 8 * c, 8), :] = piece
        wet, to_n, to_s = split(wet), split(to_n), split(to_s)
        rim = (
            jnp.where(jnp.logical_and(wet[0], small < SIDE), to_s[0], 0.0),
            jnp.where(jnp.logical_and(wet[6], small >= 102), to_n[6], 0.0),
            jnp.where(jnp.logical_and(wet[7], small < 4), to_n[7], 0.0),
        )
        for number, piece in enumerate(rim):
            rim_ref[pl.ds(pl.multiple_of(64 * number + 8 * i, 8), 8), :] = piece
        return carry

    lax.fori_loop(0, GROUPS, stencil, 0)
    fetch.wait()

    def adjoint(i, carry):
        rows = pl.ds(pl.multiple_of(8 * i, 8), 8)
        at = pl.multiple_of(64 * i, 64)
        wet = sub + 8 * i < depth
        half_x, half_y = 0.5 * wide(vel_ref, 0, rows), 0.5 * wide(vel_ref, 1, rows)
        to_e, to_w, to_n, to_s = D - half_x, D + half_x, D - half_y, D + half_y
        for t in range(2):
            answer = jnp.concatenate(
                [solved[t, pl.ds(at + 8 * c, 8), :] for c in range(CHUNKS)], axis=1
            )
            answer = jnp.where(wet, answer, 0.0)
            push_e, push_w = to_e * answer, to_w * answer
            image = mirrored(jnp.where(x29, push_e, push_w))
            moved_e, moved_w = roll(push_e, 1), roll(push_w, -1)
            straight_e = jnp.where(turned_x0, image, jnp.where(x0, 0.0, moved_e))
            straight_w = jnp.where(turned_x29, image, jnp.where(x29, 0.0, moved_w))
            cross_e = jnp.where(x0, jnp.where(turned, 0.0, moved_e), 0.0)
            cross_w = jnp.where(ends, jnp.where(turned, 0.0, moved_w), 0.0)
            inner = CENTRE * answer + straight_e + straight_w
            inner = inner + roll(to_n * answer + cross_w, SIDE)
            inner = inner + roll(to_s * answer + cross_e, -SIDE)
            inner = jnp.where(wet, inner, 0.0)
            for c, piece in enumerate(split(inner)):
                put_piece(back_ref, t, rows, c, piece)
        return carry

    lax.fori_loop(0, GROUPS, adjoint, 0)


def route_kernel(e0, e1, e2, e3, out_hbm, slots, done):
    mine = lax.shift_right_logical(lax.axis_index("tile"), 3)
    sources = (e0, e1, e2, e3)
    goals = [ref[128:129, :].astype(jnp.int32) for ref in sources]
    copies = []
    for b in range(8):
        total = jnp.zeros((128, 128), F32)
        for goal, ref in zip(goals, sources):
            total = jnp.where(goal == 8 * mine + b, ref[0:128, :], total)
        slots[b] = total
        copies.append(pltpu.make_async_copy(slots.at[b], out_hbm.at[b], done.at[b]))
        copies[-1].start()
    for copy in copies:
        copy.wait()


def finish_kernel(
    edge_ref, rhs_ref, back_hbm, rim_ref, peak_ref, link_ref,
    r0, r1, r2, r3, depth_ref, next_hbm, prev_hbm,
    right, part, solved, next_ref, prev_ref, done,
):
    fetch = pltpu.make_async_copy(back_hbm, prev_ref, done.at[2])
    fetch.start()
    depth = wide(depth_ref, slice(0, 1))
    carrier, scaled, loss = [
        sum(ref[8 * f : 8 * f + 8, :] for ref in (r0, r1, r2, r3)) for f in range(3)
    ]
    moist = scaled * jnp.exp(0.5 * peak_ref[16:24, :])
    wet = peak_ref[48:56, :] > 0.0
    heat_self = jnp.where(wet, -(0.5 * carrier + 0.25 * moist), 0.0)
    salt_heat = jnp.where(wet, 0.25 * peak_ref[24:32, :] * moist, 0.0)
    salt_self = jnp.where(wet, 0.5 * moist - loss, 0.0)
    tan_t, tan_s = peak_ref[32:40, :], peak_ref[40:48, :]
    adj_t, adj_s = peak_ref[0:8, :], peak_ref[8:16, :]

    small = lanes(8, 128)
    sub = lax.broadcasted_iota(jnp.int32, (8, WIDE), 0)

    def rims(i, carry):
        rows = pl.ds(pl.multiple_of(8 * i, 8), 8)
        at = pl.multiple_of(64 * i, 64)
        wet = split(sub + 8 * i < depth)
        rim = [rim_ref[pl.ds(pl.multiple_of(64 * n + 8 * i, 8), 8), :] for n in range(3)]
        for t in range(2):
            where = pl.ds(pl.multiple_of(64 * t + 8 * i, 8), 8)
            edge = edge_ref[0, where, :]
            for b in range(1, 8):
                edge = edge + edge_ref[b, where, :]
            north = roll(edge, 72)
            from_s, from_n = roll(edge, 68), roll(edge, 12)
            for c in range(CHUNKS):
                put = pl.ds(at + 8 * c, 8)
                value = rhs_ref[t, put, :]
                if c == 0:
                    value = value + rim[0] * edge
                elif c >= 6:
                    value = value + rim[c - 5] * north
                right[t, put, :] = value
            insides = (
                (0, jnp.logical_and(wet[0], small < SIDE), from_s),
                (6, jnp.logical_and(wet[6], small >= 102), from_n),
                (7, jnp.logical_and(wet[7], small < 4), from_n),
            )
            for c, inside, piece in insides:
                spot = slice(128 * c, min(128 * c + 128, CELLS))
                piece = jnp.where(inside, piece, 0.0)[:, 0 : spot.stop - spot.start]
                prev_ref[t, rows, spot] = prev_ref[t, rows, spot] + piece
        return carry

    fetch.wait()
    lax.fori_loop(0, GROUPS, rims, 0)
    zero = jnp.zeros((8, 128), F32)
    first = pl.ds(0, 8, stride=8)
    right[0, first, :] = right[0, first, :] + heat_self * tan_t
    right[1, first, :] = right[1, first, :] + salt_heat * tan_t + salt_self * tan_s
    adds = (heat_self * adj_t + salt_heat * adj_s, salt_self * adj_s)
    for t, add in enumerate(adds):
        for c in range(CHUNKS):
            spot = slice(128 * c, min(128 * c + 128, CELLS))
            more = add[c : c + 1, 0 : spot.stop - spot.start]
            prev_ref[t, 0:1, spot] = prev_ref[t, 0:1, spot] + more
    copy_prev = pltpu.make_async_copy(prev_ref, prev_hbm, done.at[0])
    copy_prev.start()

    def forward(i, carry):
        y_t, y_s, m = carry
        for s in range(8):
            strided = pl.ds(64 * i + s, 8, stride=8)
            packed = pl.ds(pl.multiple_of(64 * i + 8 * s, 8), 8)
            y_t = right[0, strided, :] + m * y_t
            y_s = right[1, strided, :] + m * y_s
            m = link_ref[packed, :]
            inv = link_ref[pl.ds(pl.multiple_of(512 + 64 * i + 8 * s, 8), 8), :]
            part[0, packed, :] = y_t * inv
            part[1, packed, :] = y_s * inv
        return y_t, y_s, m

    lax.fori_loop(0, GROUPS, forward, (zero, zero, zero))

    x_t = x_s = zero
    copies = [copy_prev]
    for i in reversed(range(GROUPS)):
        for s in reversed(range(8)):
            strided = pl.ds(64 * i + s, 8, stride=8)
            packed = pl.ds(64 * i + 8 * s, 8)
            m = link_ref[packed, :]
            x_t = part[0, packed, :] + m * x_t
            x_s = part[1, packed, :] + m * x_s
            solved[0, strided, :] = x_t
            solved[1, strided, :] = x_s
        rows = pl.ds(8 * i, 8)
        for t in range(2):
            for c in range(CHUNKS):
                put_piece(next_ref, t, rows, c, solved[t, pl.ds(64 * i + 8 * c, 8), :])
        copies.append(
            pltpu.make_async_copy(
                next_ref.at[:, rows, :], next_hbm.at[:, rows, :], done.at[3 + i]
            )
        )
        copies[-1].start()
    for copy in copies:
        copy.wait()


def call(kernel, name, micros, ins, outs, scratch=(), limit=VMEM_LIMIT):
    places = {"S": pltpu.SMEM, "V": pltpu.VMEM, "H": pltpu.HBM}
    shapes = [
        out if isinstance(out, jax.ShapeDtypeStruct) else jax.ShapeDtypeStruct(out, F32)
        for _, out in outs
    ]
    return pl.pallas_call(
        kernel,
        in_specs=[pl.BlockSpec(memory_space=places[place]) for place in ins],
        out_specs=[pl.BlockSpec(memory_space=places[place]) for place, _ in outs],
        out_shape=shapes,
        scratch_shapes=list(scratch),
        compiler_params=pltpu.CompilerParams(vmem_limit_bytes=limit),
        cost_estimate=pl.CostEstimate(
            flops=0, bytes_accessed=int(3.69e6 * micros), transcendentals=0
        ),
        name=name,
    )


def swap(value, axis, size, bit):
    return lax.ppermute(value, axis, [(i, i ^ bit) for i in range(size)])


def hops():
    ways = ([], [], [])
    for h in range(4):
        for low in range(2):
            step = 2 * low - 1
            targets = (((h + step) % 4, 1 - low), ((h - step) % 4, low), ((h + 2) % 4, 1 - low))
            for way, (there, low_there) in zip(ways, targets):
                for core in range(2):
                    for column in range(16):
                        source = (2 * h + core) * 32 + 2 * column + low
                        target = (2 * there + core) * 32 + 2 * column + low_there
                        way.append((source, target))
    return ways


def shards(
    tangent, adjoint, base, velocity, kappa, depth_levels, forcing, forcing_point, partner_edge,
    edge_flip,
):
    tangent, adjoint, velocity = tangent[0, 0], adjoint[0, 0], velocity[0, 0]
    base, kappa, depth = base[0, 0], kappa.reshape(Z - 1, 1, CELLS), depth_levels[0]
    mine, partner, flip = forcing_point[0], partner_edge[0], edge_flip[0]
    blocked = (2, 8 * Z, 128)
    flat = (8 * Z, 128)
    natural = (2, Z, CELLS)
    answer = (24, 128)
    line = jax.ShapeDtypeStruct((1, CELLS), jnp.int32)
    both = ("region", "tile")

    asked = [lax.ppermute(mine, both, way) for way in reversed(hops())][::-1]
    banded = forcing.reshape(8, 128, 128).transpose(1, 0, 2).reshape(1024, 128)
    edges, depth, table, solved, peak, link = call(
        solve_kernel,
        "solve",
        4.0,
        "SSHHHHHHH",
        [("V", (136, 128)), ("V", line), ("V", (384, 128))]
        + [("H", blocked), ("V", (56, 128)), ("H", (16 * Z, 128))],
        [
            pltpu.VMEM(flat, F32),
            pltpu.VMEM(blocked, F32),
            pltpu.VMEM(blocked, F32),
            pltpu.VMEM(blocked, F32),
            pltpu.VMEM((16 * Z, 128), F32),
            pltpu.VMEM(natural, F32),
            pltpu.VMEM((Z - 1, 1, CELLS), F32),
            pltpu.VMEM((1024, 128), F32),
            pltpu.VMEM(natural, F32),
            pltpu.VMEM(natural, F32),
            pltpu.VMEM((2, CELLS), F32),
            pltpu.SemaphoreType.DMA((9,)),
        ],
        limit=SOLVE_LIMIT,
    )(partner, flip, adjoint, kappa, depth, velocity, tangent, banded, base)
    table, edges, asked = lax.optimization_barrier((table, edges, asked))
    mate = swap(table, "region", 8, 1)
    edge = [edges] + [swap(edges, "tile", 32, k) for k in (8, 16, 24)]

    table, edges = lax.optimization_barrier((table, edges))
    answers = call(
        lookup_kernel,
        "lookup",
        2.7,
        "V" * 6,
        [("V", answer)] * 4,
        [pltpu.VMEM((768, 256), jnp.bfloat16)],
    )(table, mate, mine, *asked)
    replies = [answers[0]] + [
        lax.ppermute(value, both, [(target, source) for source, target in way])
        for value, way in reversed(list(zip(answers[1:], hops())))
    ]

    edge[0], first = lax.optimization_barrier((edge[0], answers[0]))
    (slots,) = call(
        route_kernel,
        "route",
        0.9,
        "VVVV",
        [("H", (8, 128, 128))],
        [pltpu.VMEM((8, 128, 128), F32), pltpu.SemaphoreType.DMA((8,))],
    )(*edge)
    groups = [[8 * a + b for b in range(8)] for a in range(4)]
    arrived = lax.all_to_all(slots, "tile", 0, 0, axis_index_groups=groups, tiled=True)

    rhs, back, rim = call(
        stencil_kernel,
        "stencil",
        3.0,
        "SVVVH",
        [("V", blocked), ("V", natural), ("V", (192, 128))],
        [pltpu.VMEM(blocked, F32), pltpu.SemaphoreType.DMA((1,))],
        limit=STENCIL_LIMIT,
    )(flip, tangent, velocity, depth, solved)

    following, previous = call(
        finish_kernel,
        "finish",
        2.1,
        "VVHVVVVVVVV",
        [("H", natural), ("H", natural)],
        [
            pltpu.VMEM(blocked, F32),
            pltpu.VMEM(blocked, F32),
            pltpu.VMEM(blocked, F32),
            pltpu.VMEM(natural, F32),
            pltpu.VMEM(natural, F32),
            pltpu.SemaphoreType.DMA((11,)),
        ],
    )(arrived, rhs, back, rim, peak, link, *replies, depth)
    return following[None, None], previous[None, None]


def solution(mesh):
    fields = P("region", "tile", None, None, None)
    rows = P("region", "tile", None, None)
    single = P("region", "tile", None)
    in_specs = (fields, fields, rows, fields, rows, single, P(None, "region"), single, single, single)
    return jax.shard_map(
        shards, mesh=mesh, in_specs=in_specs, out_specs=(fields, fields), check_vma=False
    )
```
